256 devices in a mesh: ctx: 16 (over x_hi, y, core), tp: 16 (over z, x_lo).
Axes of the slice: x: 4 (x_hi: 2, x_lo: 2; x = x_hi * 2 + x_lo), y: 4, z: 8, core: 2. Of those that a mesh axis runs over, the one named last changes fastest.
Arguments:
- queries: bfloat16 [8192, 8192], P('ctx', 'tp'), may hold values from -6 to 6
- keys: bfloat16 [8192, 8192], P('ctx', 'tp'), may hold values from -6 to 6
- values: bfloat16 [8192, 8192], P('ctx', 'tp'), may hold values from -10 to 10
- doc_ids: int32 [8192], P('ctx'), may hold values from 0 to 2, never falling along the last dimension, each value on 1 to 5120 neighbouring positions
- attn_gain: float32 [8192], P('tp'), may hold values from 0.5 to 1.5
Outputs:
- blended: bfloat16 [8192, 8192], P('ctx', 'tp')
The draws below stay inside these ranges and needn't reach their ends.
Inputs may be any that keep to these rules, and one draw needn't show every extreme that they name: doc_ids never falls along the sequence; there are three documents, each of 1 to 5120 tokens, one of exactly 5120.
All inputs are finite; a program needn't handle non-finite values.
Results may differ from the reference program's by a relative error of at most 0.0095.
Values may be sent and summed in bfloat16 or wider, within the bound.
A program may use at most 128 MiB of HBM per device.

```python
import math
import jax
import jax.numpy as jnp
import numpy as np
from jax import lax

D = 8192
HEADS = 64
HEAD_DIM = 128
SEQ = 8192
DOC_MOST = 5120


def channel_scale():
    return 10.0 ** (jnp.arange(D, dtype=jnp.float32) / (D - 1) - 0.5)


def draw_queries(key, part):
    key = jax.random.fold_in(key, 21)
    values_drawn = jnp.clip(jax.random.normal(key, (SEQ, D), jnp.float32), -6.0, 6.0)
    return values_drawn.astype(jnp.bfloat16)


def draw_keys(key, part):
    key = jax.random.fold_in(key, 31)
    values_drawn = jnp.clip(jax.random.normal(key, (SEQ, D), jnp.float32), -6.0, 6.0)
    return values_drawn.astype(jnp.bfloat16)


def draw_values(key, part):
    key = jax.random.fold_in(key, 41)
    first_key = jax.random.fold_in(key, 0)
    base_values = jax.random.normal(first_key, (SEQ, D), jnp.float32) * channel_scale()[None, :]
    return jnp.clip(base_values, -10.0, 10.0).astype(jnp.bfloat16)


def split_up(count, total, reach, slope):
    loads = [(1 << 20) // math.isqrt(standing ** slope) + 1 for standing in range(2, count + 1)]
    surplus, given = total - reach - (count - 1), [1] * (count - 1)
    while surplus > 0:
        free = [i for i in range(count - 1) if given[i] < reach]
        pool, remaining = sum([loads[i] for i in free]), surplus
        for i in free:
            extra = min(reach - given[i], max(1, remaining * loads[i] // pool), surplus)
            given[i] = given[i] + extra
            surplus = surplus - extra
    return np.array([reach] + given)


def ragged(key, amount, total, reach, skew):
    if amount == 2:
        one = jax.random.randint(key, (), max(1, total - reach), min(reach, total - 1) + 1)
        return jnp.stack([one, total - one])
    lengths = jnp.asarray(split_up(amount, total, reach, skew), jnp.int32)
    couples = (amount - 1) // 2
    donor, taker = lengths[1:1 + 2 * couples:2], lengths[2:2 + 2 * couples:2]
    margin = jnp.minimum(donor - 1, reach - taker)
    moved = jax.random.randint(jax.random.fold_in(key, 1), (couples,), 0, 1 << 20) % (margin + 1)
    lengths = lengths.at[1:1 + 2 * couples:2].set(donor - moved).at[2:2 + 2 * couples:2].set(taker + moved)
    return lengths[jax.random.permutation(jax.random.fold_in(key, 2), amount)]


def setup_inputs(seed: int = 0) -> dict:
    key_list = jax.random.split(jax.random.key(seed), 6)
    queries = draw_queries(jax.random.fold_in(key_list[5], 71), 0)
    keys = draw_keys(jax.random.fold_in(key_list[5], 71), 0)
    values = draw_values(jax.random.fold_in(key_list[5], 71), 0)
    doc_ids = jnp.searchsorted(jnp.cumsum(ragged(key_list[3], 3, SEQ, DOC_MOST, 0)), jnp.arange(SEQ), side="right").astype(jnp.int32)
    attn_gain = jnp.clip(1.0 + 0.1 * jax.random.normal(key_list[4], (D,), jnp.float32), 0.5, 1.5)
    return dict(queries=queries, keys=keys, values=values, doc_ids=doc_ids, attn_gain=attn_gain)


epsilon = 1e-06
very_low = -1e+30

def by_heads(matrix):
    return matrix.reshape(SEQ, HEADS, HEAD_DIM).transpose(1, 0, 2)

def reference(queries, keys, values, doc_ids, attn_gain):
    positions = jnp.arange(SEQ, dtype=jnp.int32)
    allowed = (positions[None, :] <= positions[:, None]) & (doc_ids[None, :] == doc_ids[:, None])
    score_scale = 1.0 / math.sqrt(HEAD_DIM)

    def one_head(triple):
        query_head, key_head, value_head = triple
        scores = jnp.dot(query_head, key_head.T, preferred_element_type=jnp.float32) * score_scale
        scores = jnp.where(allowed, scores, very_low)
        row_top = lax.optimization_barrier(jnp.max(scores, axis=1, keepdims=True))
        weights = jnp.where(allowed, jnp.exp(scores - row_top), 0.0)
        summed = lax.optimization_barrier(jnp.sum(weights, axis=1, keepdims=True))
        return jnp.dot(weights.astype(jnp.bfloat16), value_head, preferred_element_type=jnp.float32) / summed
    per_head = lax.map(one_head, (by_heads(queries), by_heads(keys), by_heads(values)))
    attention = per_head.transpose(1, 0, 2).reshape(SEQ, D)
    attn_sq = lax.optimization_barrier(jnp.sum(attention * attention, axis=1)) / D
    blended = attn_gain[None, :] * attention * lax.rsqrt(attn_sq + epsilon)[:, None]
    return blended.astype(jnp.bfloat16)
```

```python
import functools
import math

import jax
import jax.numpy as jnp
from jax import lax
from jax.experimental import pallas as pl
from jax.experimental.pallas import tpu as pltpu
from jax.sharding import PartitionSpec as P

D = 8192
HEAD_DIM = 128
CHUNK = 512
EPSILON = 1e-06
MASKED = -1e30
LOWEST = -1e20
LOG2_E = 1.4426950408889634
MESH = pl.DeviceIdType.MESH


def place():
    ctx = lax.axis_index("ctx")
    return ctx // 8, (ctx // 2) % 4, ctx % 2, lax.axis_index("tp")


def head_columns(head):
    return pl.ds(pl.multiple_of(head * HEAD_DIM, HEAD_DIM), HEAD_DIM)


def spread_kernel(q_ref, k_ref, v_ref, doc_ref, qo, ko, vo, do, q_send, q_recv, kv_send, kv_recv, fwd_send, cross_send, doc_send, doc_recv, own_sem):
    half, y, core, tp = place()
    mine = half * 8 + y * 2 + core

    barrier = pltpu.get_barrier_semaphore()
    for d in range(1, 16):
        pl.semaphore_signal(barrier, inc=1, device_id=((half * 8 + y * 2 + core + d) % 16, tp), device_id_type=MESH)
    pl.semaphore_wait(barrier, 15)

    kv = ((k_ref, ko), (v_ref, vo))

    def at(h, yy, c):
        return (h * 8 + yy * 2 + c, tp)

    started = []
    for a, (src, dst) in enumerate(kv):
        @pl.when(half == 0)
        def _():
            pltpu.make_async_remote_copy(
                src_ref=src.at[:, head_columns(y)], dst_ref=dst.at[mine], send_sem=cross_send.at[a, 0], recv_sem=kv_recv.at[a, mine],
                device_id=at(1, y, core), device_id_type=MESH).start()
    for d in (1, 3, 2):
        other = (y + d) % 4
        for a, (src, dst) in enumerate(kv):
            c = pltpu.make_async_remote_copy(
                src_ref=src.at[:, head_columns(other)], dst_ref=dst.at[mine], send_sem=kv_send.at[a, d], recv_sem=kv_recv.at[a, mine],
                device_id=at(half, other, core), device_id_type=MESH)
            c.start()
            started.append(c)
    for a, (src, dst) in enumerate(kv):
        c = pltpu.make_async_remote_copy(
            src_ref=src.at[:, head_columns(y)], dst_ref=dst.at[mine], send_sem=fwd_send.at[a, 0], recv_sem=kv_recv.at[a, mine],
            device_id=at(half, y, 1 - core), device_id_type=MESH)
        c.start()
        started.append(c)
    for d in range(1, 16):
        c = pltpu.make_async_remote_copy(
            src_ref=doc_ref, dst_ref=do.at[mine], send_sem=doc_send.at[d], recv_sem=doc_recv.at[16 - d],
            device_id=((mine + d) % 16, tp), device_id_type=MESH)
        c.start()
        started.append(c)
    for d in (1, 3, 2):
        other = (y + d) % 4
        c = pltpu.make_async_remote_copy(
            src_ref=q_ref.at[:, head_columns(other)], dst_ref=qo.at[y], send_sem=q_send.at[d], recv_sem=q_recv.at[4 - d],
            device_id=at(half, other, core), device_id_type=MESH)
        c.start()
        started.append(c)
    locals_ = [
        pltpu.make_async_copy(q_ref.at[:, head_columns(y)], qo.at[y], own_sem.at[0]),
        pltpu.make_async_copy(k_ref.at[:, head_columns(y)], ko.at[mine], own_sem.at[1]),
        pltpu.make_async_copy(v_ref.at[:, head_columns(y)], vo.at[mine], own_sem.at[2]),
        pltpu.make_async_copy(doc_ref, do.at[mine], own_sem.at[3]),
    ]
    for c in locals_:
        c.start()

    def landed(a, slot):
        dst = kv[a][1]
        pltpu.make_async_remote_copy(
            src_ref=dst.at[slot], dst_ref=dst.at[slot], send_sem=kv_send.at[a, 0], recv_sem=kv_recv.at[a, slot],
            device_id=at(half, y, 1 - core), device_id_type=MESH).wait_recv()

    for n, d in enumerate((1, 3, 2)):
        slot = half * 8 + ((y + d) % 4) * 2 + core
        for a in range(2):
            dst = kv[a][1]
            landed(a, slot)

            @pl.when(half == 0)
            def _():
                pltpu.make_async_remote_copy(
                    src_ref=dst.at[slot], dst_ref=dst.at[slot], send_sem=cross_send.at[a, n + 1], recv_sem=kv_recv.at[a, slot],
                    device_id=at(1, y, core), device_id_type=MESH).start()
            c = pltpu.make_async_remote_copy(
                src_ref=dst.at[slot], dst_ref=dst.at[slot], send_sem=fwd_send.at[a, n + 1], recv_sem=kv_recv.at[a, slot],
                device_id=at(half, y, 1 - core), device_id_type=MESH)
            c.start()
            started.append(c)

    order = (0, 1, 3, 2)
    @pl.when(half == 1)
    def _():
        for n, d in enumerate(order):
            slot = ((y + d) % 4) * 2 + core
            for a in range(2):
                dst = kv[a][1]
                landed(a, slot)
                pltpu.make_async_remote_copy(
                    src_ref=dst.at[slot], dst_ref=dst.at[slot], send_sem=cross_send.at[a, n], recv_sem=kv_recv.at[a, slot],
                    device_id=at(1, y, 1 - core), device_id_type=MESH).start()
        for n, d in enumerate(order):
            for a in range(2):
                landed(a, ((y + d) % 4) * 2 + 1 - core)

    for d in range(4):
        for a in range(2):
            landed(a, half * 8 + ((y + d) % 4) * 2 + 1 - core)
    for n in range(4):
        for a in range(2):
            dst = kv[a][1]
            pltpu.make_async_remote_copy(
                src_ref=dst.at[mine], dst_ref=dst.at[mine], send_sem=cross_send.at[a, n], recv_sem=kv_recv.at[a, mine],
                device_id=at(half, y, 1 - core), device_id_type=MESH).wait_send()
    for d in (1, 2, 3):
        pltpu.make_async_remote_copy(
            src_ref=qo.at[y], dst_ref=qo.at[y], send_sem=q_send.at[d], recv_sem=q_recv.at[d],
            device_id=at(half, y, 1 - core), device_id_type=MESH).wait_recv()
    for d in range(1, 16):
        pltpu.make_async_remote_copy(
            src_ref=doc_ref, dst_ref=do.at[mine], send_sem=doc_send.at[d], recv_sem=doc_recv.at[d],
            device_id=at(half, y, 1 - core), device_id_type=MESH).wait_recv()
    for c in started:
        c.wait_send()
    for c in locals_:
        c.wait()


def spread(queries, keys, values, docs):
    hbm = pl.BlockSpec(memory_space=pltpu.HBM)
    return pl.pallas_call(
        spread_kernel,
        name="spread",
        out_shape=[
            jax.ShapeDtypeStruct((4, CHUNK, HEAD_DIM), jnp.bfloat16),
            jax.ShapeDtypeStruct((16, CHUNK, HEAD_DIM), jnp.bfloat16),
            jax.ShapeDtypeStruct((16, CHUNK, HEAD_DIM), jnp.bfloat16),
            jax.ShapeDtypeStruct((16, 4, 128), jnp.int32),
        ],
        in_specs=[hbm] * 4,
        out_specs=[hbm] * 4,
        scratch_shapes=[
            pltpu.SemaphoreType.DMA((4,)),
            pltpu.SemaphoreType.DMA((4,)),
            pltpu.SemaphoreType.DMA((2, 4)),
            pltpu.SemaphoreType.DMA((2, 16)),
            pltpu.SemaphoreType.DMA((2, 4)),
            pltpu.SemaphoreType.DMA((2, 4)),
            pltpu.SemaphoreType.DMA((16,)),
            pltpu.SemaphoreType.DMA((16,)),
            pltpu.SemaphoreType.DMA((4,)),
        ],
        compiler_params=pltpu.CompilerParams(collective_id=0, has_side_effects=True),
    )(queries, keys, values, docs)


def attend_kernel(q_ref, k_ref, v_ref, doc_ref, o_ref):
    half, y, core, tp = place()
    scale = LOG2_E / math.sqrt(HEAD_DIM)
    seen = lax.broadcasted_iota(jnp.int32, (16, 4, 128), 0) < half * 8 + 8
    docs = doc_ref[...]
    first = jnp.sum(jnp.where(seen & (docs < 1), 1, 0))
    second = jnp.sum(jnp.where(seen & (docs < 2), 1, 0))

    def start_of(t):
        return jnp.where(t >= second, second, jnp.where(t >= first, first, 0))

    for n in range(4):
        chunk = half * 8 + n * 2 + core
        t0 = chunk * CHUNK
        q = q_ref[n]
        low = start_of(t0)
        high = start_of(t0 + CHUNK - 1)
        low_block = low // CHUNK
        whole = jnp.maximum(jnp.minimum((high + CHUNK - 1) // CHUNK, chunk), low_block)

        def block(k, state, masked):
            top, total, acc = state
            s = lax.dot_general(q, k_ref[k], (((1,), (1,)), ((), ())), preferred_element_type=jnp.float32) * scale
            if masked:
                rows = t0 + lax.broadcasted_iota(jnp.int32, (CHUNK, 1), 0)
                begin = start_of(rows)
                cols = k * CHUNK + lax.broadcasted_iota(jnp.int32, (CHUNK, CHUNK), 1)
                s = jnp.where((cols <= rows) & (cols >= begin), s, MASKED)
            new_top = jnp.maximum(top, jnp.max(s, axis=1, keepdims=True))
            p = jnp.exp2(s - new_top)
            factor = jnp.exp2(top - new_top)
            part = p[:, :128]
            for g in range(1, CHUNK // 128):
                part = part + p[:, g * 128:(g + 1) * 128]
            total = total * factor + part
            acc = acc * factor + jnp.dot(p.astype(jnp.bfloat16), v_ref[k], preferred_element_type=jnp.float32)
            return new_top, total, acc

        state = (jnp.full((CHUNK, 1), LOWEST, jnp.float32), jnp.zeros((CHUNK, 128), jnp.float32), jnp.zeros((CHUNK, HEAD_DIM), jnp.float32))
        state = lax.fori_loop(low_block, whole, lambda k, s: block(k, s, True), state)
        state = lax.fori_loop(whole, chunk, lambda k, s: block(k, s, False), state)
        top, total, acc = block(chunk, state, True)
        o_ref[n] = (acc / jnp.sum(total, axis=1, keepdims=True)).astype(jnp.bfloat16)


def attend(q, k, v, docs):
    return pl.pallas_call(
        attend_kernel,
        name="attend",
        out_shape=jax.ShapeDtypeStruct((4, CHUNK, HEAD_DIM), jnp.bfloat16),
        in_specs=[pl.BlockSpec(memory_space=pltpu.VMEM)] * 4,
        out_specs=pl.BlockSpec(memory_space=pltpu.VMEM),
        compiler_params=pltpu.CompilerParams(vmem_limit_bytes=48 * 1024 * 1024),
        cost_estimate=pl.CostEstimate(flops=3 * 10**9, bytes_accessed=5 * 2**20, transcendentals=6 * 10**6),
    )(q, k, v, docs)


def collect_kernel(o_ref, rows_ref, sums_ref, square, squares, o_send, o_recv, s_send, s_recv, own_sem):
    half, y, core, tp = place()

    barrier = pltpu.get_barrier_semaphore()
    for d in range(1, 4):
        pl.semaphore_signal(barrier, inc=1, device_id=(half * 8 + ((y + d) % 4) * 2 + core, tp), device_id_type=MESH)
    for d in range(1, 16):
        pl.semaphore_signal(barrier, inc=1, device_id=(half * 8 + y * 2 + core, (tp + d) % 16), device_id_type=MESH)
    pl.semaphore_wait(barrier, 18)

    sends = []
    for d in (2, 1, 3):
        other = (y + d) % 4
        c = pltpu.make_async_remote_copy(
            src_ref=o_ref.at[other], dst_ref=rows_ref.at[:, head_columns(y)], send_sem=o_send.at[d], recv_sem=o_recv.at[4 - d],
            device_id=(half * 8 + other * 2 + core, tp), device_id_type=MESH)
        c.start()
        sends.append(c)
    own = pltpu.make_async_copy(o_ref.at[y], rows_ref.at[:, head_columns(y)], own_sem.at[0])
    own.start()

    def add(head, sums):
        x = rows_ref[:, head_columns(head)].astype(jnp.float32)
        return sums + lax.dot_general(
            jnp.ones((8, HEAD_DIM), jnp.float32), x * x, (((1,), (1,)), ((), ())),
            precision=lax.Precision.HIGHEST, preferred_element_type=jnp.float32)

    own.wait()
    sums = add(y, jnp.zeros((8, CHUNK), jnp.float32))
    for d in (1, 3, 2):
        pltpu.make_async_remote_copy(
            src_ref=o_ref.at[y], dst_ref=rows_ref.at[:, head_columns((y + d) % 4)], send_sem=o_send.at[d], recv_sem=o_recv.at[d],
            device_id=(half * 8 + y * 2 + core, tp), device_id_type=MESH).wait_recv()
        sums = add((y + d) % 4, sums)
    square[...] = sums[:1]
    for d in range(1, 16):
        c = pltpu.make_async_remote_copy(
            src_ref=square, dst_ref=squares.at[tp], send_sem=s_send.at[d], recv_sem=s_recv.at[16 - d],
            device_id=(half * 8 + y * 2 + core, (tp + d) % 16), device_id_type=MESH)
        c.start()
        sends.append(c)
    total = square[...]
    for d in range(1, 16):
        pltpu.make_async_remote_copy(
            src_ref=square, dst_ref=squares.at[(tp + d) % 16], send_sem=s_send.at[d], recv_sem=s_recv.at[d],
            device_id=(half * 8 + y * 2 + core, tp), device_id_type=MESH).wait_recv()
    for d in range(1, 16):
        total = total + squares[(tp + d) % 16]
    sums_ref[...] = lax.rsqrt(total * (1.0 / D) + EPSILON)
    for c in sends:
        c.wait_send()


def collect(o):
    return pl.pallas_call(
        collect_kernel,
        name="collect",
        out_shape=[
            jax.ShapeDtypeStruct((CHUNK, 4 * HEAD_DIM), jnp.bfloat16),
            jax.ShapeDtypeStruct((1, CHUNK), jnp.float32),
        ],
        in_specs=[pl.BlockSpec(memory_space=pltpu.VMEM)],
        out_specs=[pl.BlockSpec(memory_space=pltpu.VMEM)] * 2,
        scratch_shapes=[
            pltpu.VMEM((1, CHUNK), jnp.float32),
            pltpu.VMEM((16, 1, CHUNK), jnp.float32),
            pltpu.SemaphoreType.DMA((4,)),
            pltpu.SemaphoreType.DMA((4,)),
            pltpu.SemaphoreType.DMA((16,)),
            pltpu.SemaphoreType.DMA((16,)),
            pltpu.SemaphoreType.DMA((1,)),
        ],
        compiler_params=pltpu.CompilerParams(collective_id=1, has_side_effects=True),
    )(o)


def local(queries, keys, values, doc_ids, attn_gain):
    q, k, v, docs = spread(queries, keys, values, doc_ids.reshape(4, 128))
    o = attend(q, k, v, docs)
    rows, factor = collect(o)
    blended = attn_gain[None, :] * rows.astype(jnp.float32) * factor.reshape(CHUNK, 1)
    return blended.astype(jnp.bfloat16)


def solution(mesh):
    placed = (P("ctx", "tp"), P("ctx", "tp"), P("ctx", "tp"), P("ctx"), P("tp"))
    return jax.shard_map(
        local, mesh=mesh, in_specs=placed, out_specs=P("ctx", "tp"), check_vma=False
    )
```

```python
import math

import jax
import jax.numpy as jnp
from jax import lax
from jax.experimental import pallas as pl
from jax.experimental.pallas import tpu as pltpu
from jax.sharding import PartitionSpec as P

D = 8192
HEAD_DIM = 128
CHUNK = 512
REACH = 5
EPSILON = 1e-06
MASKED = -1e29
LOWEST = -1e20
OTHER_DOC = -(2.0**100)
SCALE = 1.4426950408889634 / math.sqrt(HEAD_DIM)
ROWS = HEAD_DIM + 16
MESH = pl.DeviceIdType.MESH


def head_columns(head):
    return pl.ds(pl.multiple_of(head * HEAD_DIM, HEAD_DIM), HEAD_DIM)


def fused_kernel(
    q_ref, k_ref, v_ref, doc_ref, rows_ref, factor_ref,
    qbuf, kbuf, vbuf, docs, qfeat, kfeat, vt, sbuf, acc, top, obuf, part, parts, square, squares,
    q_send, q_recv, kv_send, kv_recv, fwd_send, cross_send, doc_send, doc_recv, own_sem,
    o_send, o_recv, p_send, p_recv, s_send, s_recv,
):
    ctx, tp = lax.axis_index("ctx"), lax.axis_index("tp")
    half, y, core = ctx // 8, (ctx // 2) % 4, ctx % 2
    mine = half * 8 + y * 2 + core

    def at(h, yy, c):
        return (h * 8 + yy * 2 + c, tp)

    sibling = at(half, y, 1 - core)

    barrier = pltpu.get_barrier_semaphore()
    for d in range(1, 16):
        pl.semaphore_signal(barrier, inc=1, device_id=((mine + d) % 16, tp), device_id_type=MESH)
    for d in range(1, 16):
        pl.semaphore_signal(barrier, inc=1, device_id=(mine, (tp + d) % 16), device_id_type=MESH)
    pl.semaphore_wait(barrier, 30)

    kv = ((k_ref, kbuf), (v_ref, vbuf))

    def remote(src, dst, send, recv, device):
        return pltpu.make_async_remote_copy(src_ref=src, dst_ref=dst, send_sem=send, recv_sem=recv, device_id=device, device_id_type=MESH)

    def doc_copy(d):
        return remote(doc_ref, docs.at[mine], doc_send.at[d], doc_recv.at[16 - d], ((mine + d) % 16, tp))

    def q_copy(d):
        other = (y + d) % 4
        return remote(q_ref.at[:, head_columns(other)], qbuf.at[y], q_send.at[d], q_recv.at[4 - d], at(half, other, core))

    def kv_copy(a, d):
        other = (y + d) % 4
        return remote(kv[a][0].at[:, head_columns(other)], kv[a][1].at[mine], kv_send.at[a, d], kv_recv.at[a, mine], at(half, other, core))

    def own_copy(a, send, device):
        return remote(kv[a][0].at[:, head_columns(y)], kv[a][1].at[mine], send, kv_recv.at[a, mine], device)

    def pass_on(a, slot, send, device):
        return remote(kv[a][1].at[slot], kv[a][1].at[slot], send, kv_recv.at[a, slot], device)

    def landed(slot):
        for a in range(2):
            pass_on(a, slot, kv_send.at[a, 0], sibling).wait_recv()

    for d in range(1, 16):
        doc_copy(d).start()
    locals_ = [
        pltpu.make_async_copy(doc_ref, docs.at[mine], own_sem.at[0]),
        pltpu.make_async_copy(q_ref.at[:, head_columns(y)], qbuf.at[y], own_sem.at[1]),
        pltpu.make_async_copy(k_ref.at[:, head_columns(y)], kbuf.at[mine], own_sem.at[2]),
        pltpu.make_async_copy(v_ref.at[:, head_columns(y)], vbuf.at[mine], own_sem.at[3]),
    ]
    for c in locals_:
        c.start()

    @pl.when(half == 0)
    def _():
        for a in range(2):
            own_copy(a, cross_send.at[a, 0], at(1, y, core)).start()
        for d in (1, 3, 2):
            for a in range(2):
                kv_copy(a, d).start()
        for d in (1, 3, 2):
            q_copy(d).start()

    @pl.when(half == 1)
    def _():
        for d in (1, 3, 2):
            q_copy(d).start()
        for d in (1, 3, 2):
            for a in range(2):
                kv_copy(a, d).start()

    for a in range(2):
        own_copy(a, fwd_send.at[a, 0], sibling).start()

    acc[...] = jnp.zeros(acc.shape, jnp.float32)
    top[...] = jnp.full(top.shape, LOWEST, jnp.float32)
    vt[:, HEAD_DIM:, :] = jnp.ones((2, ROWS - HEAD_DIM, CHUNK), jnp.bfloat16)

    for d in range(1, 16):
        remote(doc_ref, docs.at[mine], doc_send.at[d], doc_recv.at[d], sibling).wait_recv()
    for c in locals_:
        c.wait()

    def count(below):
        ones = jnp.where(docs[...] < below, 1.0, 0.0)
        return jnp.sum(jnp.sum(jnp.sum(ones, axis=0), axis=0, keepdims=True), axis=1, keepdims=True)

    second, third = count(1), count(2)
    lane = lax.broadcasted_iota(jnp.int32, (CHUNK, HEAD_DIM), 1)

    def doc_of(chunk):
        t = (chunk * CHUNK + lax.broadcasted_iota(jnp.int32, (CHUNK, HEAD_DIM), 0)).astype(jnp.float32)
        return jnp.where(t >= third, 2, jnp.where(t >= second, 1, 0))

    def key_features(s, _):
        kfeat[s] = jnp.where((lane < 3) & (lane != doc_of(s)), OTHER_DOC, 0.0).astype(jnp.bfloat16)
        return 0

    lax.fori_loop(0, half * 8 + 8, key_features, 0)

    def query_features(n, _):
        qfeat[n] = jnp.where(lane == doc_of(half * 8 + n * 2 + core), 1.0, 0.0).astype(jnp.bfloat16)
        return 0

    lax.fori_loop(0, 4, query_features, 0)

    @pl.when(half == 0)
    def _():
        for n, d in enumerate((1, 3, 2)):
            slot = ((y + d) % 4) * 2 + core
            landed(slot)
            for a in range(2):
                pass_on(a, slot, cross_send.at[a, n + 1], at(1, y, core)).start()
                pass_on(a, slot, fwd_send.at[a, n + 1], sibling).start()

    for d in (1, 3, 2):
        remote(qbuf.at[y], qbuf.at[y], q_send.at[d], q_recv.at[d], sibling).wait_recv()

    def score(slot, n):
        k = jnp.concatenate([kbuf[slot], kfeat[slot]], axis=1)
        q = jnp.concatenate([qbuf[n], qfeat[n]], axis=1)
        return lax.dot_general(k, q, (((1,), (1,)), ((), ())), preferred_element_type=jnp.float32) * SCALE

    def put_score(slot, n, buf):
        s = score(slot, n)
        sbuf[buf] = s
        return jnp.max(s, axis=0, keepdims=True)

    def absorb(state, s, s_top, buf):
        t, a = state
        new = jnp.maximum(t, s_top)
        p = jnp.exp2(s - new).astype(jnp.bfloat16)
        return new, a * jnp.exp2(t - new) + jnp.dot(vt[buf], p, preferred_element_type=jnp.float32)

    def visit(v, _):
        j, kind = v // (1 + half), v % (1 + half)
        d = j + j // 2 - 2 * (j // 3)
        pair = (y + d) % 4 + 4 * half * (1 - kind)
        slot_a, slot_b = pair * 2 + core, pair * 2 + 1 - core

        @pl.when((half == 1) & (v > 0))
        def _():
            landed(slot_a)
            for a in range(2):
                pass_on(a, slot_a, fwd_send.at[a, v], sibling).start()

        vt[0, :HEAD_DIM, :] = vbuf[slot_a].T
        landed(slot_b)
        vt[1, :HEAD_DIM, :] = vbuf[slot_b].T

        first = jnp.maximum(pair - 4 * half, 0)
        last = jnp.minimum(pair + REACH - 4 * half, 3)

        @pl.when(kind == 0)
        def _():
            s = score(slot_a, first)
            key = lax.broadcasted_iota(jnp.int32, (CHUNK, CHUNK), 0)
            query = lax.broadcasted_iota(jnp.int32, (CHUNK, CHUNK), 1)
            s = jnp.where(key <= query, s, MASKED)
            t, a = absorb((top[first], acc[first]), s, jnp.max(s, axis=0, keepdims=True), 0)
            top[first] = t
            acc[first] = a

            @pl.when(core == 1)
            def _():
                s = score(slot_b, first)
                t, a = absorb((top[first], acc[first]), s, jnp.max(s, axis=0, keepdims=True), 1)
                top[first] = t
                acc[first] = a

        begin = first + 1 - kind

        @pl.when(begin <= last)
        def _():
            def task(n, top_a):
                state = (top[n], acc[n])
                top_b = put_score(slot_b, n, 1)
                state = absorb(state, sbuf[0], top_a, 0)
                top_a = put_score(slot_a, jnp.minimum(n + 1, last), 0)
                t, a = absorb(state, sbuf[1], top_b, 1)
                top[n] = t
                acc[n] = a
                return top_a

            lax.fori_loop(begin, last + 1, task, put_score(slot_a, begin, 0))

        return 0

    lax.fori_loop(0, 4 + 4 * half, visit, 0)

    def o_copy(n):
        return remote(obuf.at[n], rows_ref.at[:, head_columns(y)], o_send.at[n], o_recv.at[y], at(half, n, core))

    def p_copy(n):
        return remote(part.at[n], parts.at[y], p_send.at[n], p_recv.at[y], at(half, n, core))

    def finish(n, _):
        a = acc[n]
        o = a[:HEAD_DIM] / a[HEAD_DIM:HEAD_DIM + 1]
        part[n] = jnp.sum(o * o, axis=0, keepdims=True)
        obuf[n] = o.T.astype(jnp.bfloat16)

        @pl.when(n != y)
        def _():
            p_copy(n).start()
            o_copy(n).start()
        return 0

    lax.fori_loop(0, 4, finish, 0)
    own = pltpu.make_async_copy(obuf.at[y], rows_ref.at[:, head_columns(y)], own_sem.at[4])
    own.start()
    total = part[y]
    for d in (1, 3, 2):
        other = (y + d) % 4
        remote(part.at[y], parts.at[other], p_send.at[y], p_recv.at[other], sibling).wait_recv()
        total = total + parts[other]
    square[...] = total

    def s_copy(d):
        return remote(square, squares.at[tp], s_send.at[d], s_recv.at[16 - d], (mine, (tp + d) % 16))

    for d in range(1, 16):
        s_copy(d).start()
    for d in range(1, 16):
        other = (tp + d) % 16
        remote(square, squares.at[other], s_send.at[d], s_recv.at[d], sibling).wait_recv()
        total = total + squares[other]
    factor_ref[...] = lax.rsqrt(total * (1.0 / D) + EPSILON)

    own.wait()
    for d in (1, 3, 2):
        other = (y + d) % 4
        remote(obuf.at[y], rows_ref.at[:, head_columns(other)], o_send.at[y], o_recv.at[other], sibling).wait_recv()
        o_copy(other).wait_send()
        p_copy(other).wait_send()
        q_copy(d).wait_send()
        for a in range(2):
            kv_copy(a, d).wait_send()
    for d in range(1, 16):
        s_copy(d).wait_send()
        doc_copy(d).wait_send()

    def sent(v, _):
        for a in range(2):
            pass_on(a, mine, fwd_send.at[a, v], sibling).wait_send()
        return 0

    lax.fori_loop(0, 4 + 4 * half, sent, 0)

    @pl.when(half == 0)
    def _():
        for n in range(4):
            for a in range(2):
                pass_on(a, mine, cross_send.at[a, n], sibling).wait_send()


def fused(queries, keys, values, docs):
    hbm = pl.BlockSpec(memory_space=pltpu.HBM)
    vmem = pl.BlockSpec(memory_space=pltpu.VMEM)
    dma = pltpu.SemaphoreType.DMA
    bf16, f32 = jnp.bfloat16, jnp.float32
    return pl.pallas_call(
        fused_kernel,
        name="fused",
        out_shape=[
            jax.ShapeDtypeStruct((CHUNK, 4 * HEAD_DIM), bf16),
            jax.ShapeDtypeStruct((1, CHUNK), f32),
        ],
        in_specs=[hbm] * 4,
        out_specs=[vmem] * 2,
        scratch_shapes=[
            pltpu.VMEM((4, CHUNK, HEAD_DIM), bf16),
            pltpu.VMEM((16, CHUNK, HEAD_DIM), bf16),
            pltpu.VMEM((16, CHUNK, HEAD_DIM), bf16),
            pltpu.VMEM((16, 4, 128), jnp.int32),
            pltpu.VMEM((4, CHUNK, HEAD_DIM), bf16),
            pltpu.VMEM((16, CHUNK, HEAD_DIM), bf16),
            pltpu.VMEM((2, ROWS, CHUNK), bf16),
            pltpu.VMEM((2, CHUNK, CHUNK), f32),
            pltpu.VMEM((4, ROWS, CHUNK), f32),
            pltpu.VMEM((4, 1, CHUNK), f32),
            pltpu.VMEM((4, CHUNK, HEAD_DIM), bf16),
            pltpu.VMEM((4, 1, CHUNK), f32),
            pltpu.VMEM((4, 1, CHUNK), f32),
            pltpu.VMEM((1, CHUNK), f32),
            pltpu.VMEM((16, 1, CHUNK), f32),
            dma((4,)), dma((4,)), dma((2, 4)), dma((2, 16)), dma((2, 8)), dma((2, 4)), dma((16,)), dma((16,)), dma((5,)),
            dma((4,)), dma((4,)), dma((4,)), dma((4,)), dma((16,)), dma((16,)),
        ],
        compiler_params=pltpu.CompilerParams(collective_id=0, has_side_effects=True, vmem_limit_bytes=40 * 2**20),
    )(queries, keys, values, docs)


def local(queries, keys, values, doc_ids, attn_gain):
    rows, factor = fused(queries, keys, values, doc_ids.reshape(4, 128))
    blended = attn_gain[None, :] * rows.astype(jnp.float32) * factor.reshape(CHUNK, 1)
    return blended.astype(jnp.bfloat16)


def solution(mesh):
    placed = (P("ctx", "tp"), P("ctx", "tp"), P("ctx", "tp"), P("ctx"), P("tp"))
    return jax.shard_map(
        local, mesh=mesh, in_specs=placed, out_specs=P("ctx", "tp"), check_vma=False
    )
```

```python
import math

import jax
import jax.numpy as jnp
from jax import lax
from jax.experimental import pallas as pl
from jax.experimental.pallas import tpu as pltpu
from jax.sharding import PartitionSpec as P

D = 8192
HEAD_DIM = 128
CHUNK = 512
REACH = 5
EPSILON = 1e-06
MASKED = -1e29
LOWEST = -1e20
OTHER_DOC = -(2.0**100)
SCALE = 1.4426950408889634 / math.sqrt(HEAD_DIM)
ROWS = HEAD_DIM + 16
MESH = pl.DeviceIdType.MESH


def head_columns(head):
    return pl.ds(pl.multiple_of(head * HEAD_DIM, HEAD_DIM), HEAD_DIM)


def fused_kernel(
    q_ref, k_ref, v_ref, doc_ref, rows_ref, factor_ref,
    qbuf, kbuf, vbuf, docs, qfeat, kfeat, vt, sbuf, acc, top, obuf, part, parts, square, squares,
    q_send, q_recv, kv_send, kv_recv, fwd_send, cross_send, doc_send, doc_recv, own_sem,
    o_send, o_recv, p_send, p_recv, s_send, s_recv,
):
    ctx, tp = lax.axis_index("ctx"), lax.axis_index("tp")
    half, y, core = ctx // 8, (ctx // 2) % 4, ctx % 2
    mine = half * 8 + y * 2 + core

    def at(h, yy, c):
        return (h * 8 + yy * 2 + c, tp)

    sibling = at(half, y, 1 - core)

    barrier = pltpu.get_barrier_semaphore()
    for d in range(1, 16):
        pl.semaphore_signal(barrier, inc=1, device_id=((mine + d) % 16, tp), device_id_type=MESH)
    for d in range(1, 16):
        pl.semaphore_signal(barrier, inc=1, device_id=(mine, (tp + d) % 16), device_id_type=MESH)
    pl.semaphore_wait(barrier, 30)

    kv = ((k_ref, kbuf), (v_ref, vbuf))

    def remote(src, dst, send, recv, device):
        return pltpu.make_async_remote_copy(src_ref=src, dst_ref=dst, send_sem=send, recv_sem=recv, device_id=device, device_id_type=MESH)

    def doc_copy(d):
        return remote(doc_ref, docs.at[mine], doc_send.at[d], doc_recv.at[16 - d], ((mine + d) % 16, tp))

    def q_copy(d):
        other = (y + d) % 4
        return remote(q_ref.at[:, head_columns(other)], qbuf.at[y], q_send.at[d], q_recv.at[4 - d], at(half, other, core))

    def kv_copy(a, d):
        other = (y + d) % 4
        return remote(kv[a][0].at[:, head_columns(other)], kv[a][1].at[mine], kv_send.at[a, d], kv_recv.at[a, mine], at(half, other, core))

    def own_copy(a, send, device):
        return remote(kv[a][0].at[:, head_columns(y)], kv[a][1].at[mine], send, kv_recv.at[a, mine], device)

    def pass_on(a, slot, send, device):
        return remote(kv[a][1].at[slot], kv[a][1].at[slot], send, kv_recv.at[a, slot], device)

    def landed(slot):
        for a in range(2):
            pass_on(a, slot, kv_send.at[a, 0], sibling).wait_recv()

    for d in range(1, 16):
        doc_copy(d).start()
    locals_ = [
        pltpu.make_async_copy(doc_ref, docs.at[mine], own_sem.at[0]),
        pltpu.make_async_copy(q_ref.at[:, head_columns(y)], qbuf.at[y], own_sem.at[1]),
        pltpu.make_async_copy(k_ref.at[:, head_columns(y)], kbuf.at[mine], own_sem.at[2]),
        pltpu.make_async_copy(v_ref.at[:, head_columns(y)], vbuf.at[mine], own_sem.at[3]),
    ]
    for c in locals_:
        c.start()

    @pl.when(half == 0)
    def _():
        for a in range(2):
            own_copy(a, cross_send.at[a, 0], at(1, y, core)).start()
        for d in (1, 3):
            for a in range(2):
                kv_copy(a, d).start()

    @pl.when(half == 1)
    def _():
        for d in (1, 3, 2):
            q_copy(d).start()

    for a in range(2):
        own_copy(a, fwd_send.at[a, 0], sibling).start()

    acc[...] = jnp.zeros(acc.shape, jnp.float32)
    top[...] = jnp.full(top.shape, LOWEST, jnp.float32)

    def ones_rows(n, _):
        vt[n, HEAD_DIM:, :] = jnp.ones((ROWS - HEAD_DIM, CHUNK), jnp.bfloat16)
        return 0

    lax.fori_loop(0, 8 + 8 * half, ones_rows, 0)

    for d in range(1, 16):
        remote(doc_ref, docs.at[mine], doc_send.at[d], doc_recv.at[d], sibling).wait_recv()
    for c in locals_:
        c.wait()

    def count(below):
        ones = jnp.where(docs[...] < below, 1.0, 0.0)
        return jnp.sum(jnp.sum(jnp.sum(ones, axis=0), axis=0, keepdims=True), axis=1, keepdims=True)

    second, third = count(1), count(2)
    lane = lax.broadcasted_iota(jnp.int32, (CHUNK, HEAD_DIM), 1)

    def doc_of(chunk):
        t = (chunk * CHUNK + lax.broadcasted_iota(jnp.int32, (CHUNK, HEAD_DIM), 0)).astype(jnp.float32)
        return jnp.where(t >= third, 2, jnp.where(t >= second, 1, 0))

    def key_features(s, _):
        kfeat[s] = jnp.where((lane < 3) & (lane != doc_of(s)), OTHER_DOC, 0.0).astype(jnp.bfloat16)
        return 0

    lax.fori_loop(0, half * 8 + 8, key_features, 0)

    def query_features(n, _):
        qfeat[n] = jnp.where(lane == doc_of(half * 8 + n * 2 + core), 1.0, 0.0).astype(jnp.bfloat16)
        return 0

    lax.fori_loop(0, 4, query_features, 0)

    def along(j):
        return j + j // 2 - 2 * (j // 3)

    falling = ((y + 1) // 2 + 1) % 2
    swapped = (y // 2) * (1 - falling)

    def across(j):
        return falling * ((4 - j) % 4) + (1 - falling) * (j + swapped * (j // 2) * (5 - 2 * j))

    def pass_to_sibling(slot, n):
        for a in range(2):
            pass_on(a, slot, fwd_send.at[a, n], sibling).start()

    def turn(slot):
        vt[slot, :HEAD_DIM, :] = vbuf[slot].T

    def q_landed(d):
        remote(qbuf.at[y], qbuf.at[y], q_send.at[0], q_recv.at[d], sibling).wait_recv()

    def score(slot, n):
        k = jnp.concatenate([kbuf[slot], kfeat[slot]], axis=1)
        q = jnp.concatenate([qbuf[n], qfeat[n]], axis=1)
        return lax.dot_general(k, q, (((1,), (1,)), ((), ())), preferred_element_type=jnp.float32) * SCALE

    def put_score(slot, n, buf):
        s = score(slot, n)
        sbuf[buf] = s
        return jnp.max(s, axis=0, keepdims=True)

    def absorb(state, s, s_top, slot):
        t, a = state
        new = jnp.maximum(t, s_top)
        p = jnp.exp2(s - new).astype(jnp.bfloat16)
        return new, a * jnp.exp2(t - new) + jnp.dot(vt[slot], p, preferred_element_type=jnp.float32)

    def diagonal(slot_a, slot_b, n):
        def masked():
            key = lax.broadcasted_iota(jnp.int32, (CHUNK, CHUNK), 0)
            query = lax.broadcasted_iota(jnp.int32, (CHUNK, CHUNK), 1)
            return jnp.where(key <= query, score(slot_a, n), MASKED)

        @pl.when(core == 0)
        def _():
            s = masked()
            t, a = absorb((top[n], acc[n]), s, jnp.max(s, axis=0, keepdims=True), slot_a)
            top[n] = t
            acc[n] = a

        @pl.when(core == 1)
        def _():
            s_b, s_a = score(slot_b, n), masked()
            t = top[n]
            new = jnp.maximum(t, jnp.maximum(jnp.max(s_a, axis=0, keepdims=True), jnp.max(s_b, axis=0, keepdims=True)))
            p_b = jnp.exp2(s_b - new).astype(jnp.bfloat16)
            p_a = jnp.exp2(s_a - new).astype(jnp.bfloat16)
            top[n] = new
            acc[n] = (
                acc[n] * jnp.exp2(t - new)
                + jnp.dot(vt[slot_b], p_b, preferred_element_type=jnp.float32)
                + jnp.dot(vt[slot_a], p_a, preferred_element_type=jnp.float32)
            )

    def whole(slot_a, slot_b, n, next_a, next_n, top_a):
        state = (top[n], acc[n])
        top_b = put_score(slot_b, n, 1)
        state = absorb(state, sbuf[0], top_a, slot_a)
        top_a = put_score(next_a, next_n, 0)
        t, a = absorb(state, sbuf[1], top_b, slot_b)
        top[n] = t
        acc[n] = a
        return top_a

    def o_copy(n):
        return remote(obuf.at[n], rows_ref.at[:, head_columns(y)], o_send.at[n], o_recv.at[y], at(half, n, core))

    def p_copy(n):
        return remote(part.at[n], parts.at[y], p_send.at[n], p_recv.at[y], at(half, n, core))

    def finish(n, _):
        a = acc[n]
        o = a[:HEAD_DIM] / a[HEAD_DIM:HEAD_DIM + 1]
        part[n] = jnp.sum(o * o, axis=0, keepdims=True)
        obuf[n] = o.T.astype(jnp.bfloat16)

        @pl.when(n != y)
        def _():
            p_copy(n).start()
            o_copy(n).start()
        return 0

    @pl.when(half == 0)
    def _():
        turn(mine)
        for d in (1, 3):
            for a in range(2):
                kv_copy(a, d).wait_send()
        for a in range(2):
            kv_copy(a, 2).start()

        def relay(j, _):
            slot = ((y + across(j)) % 4) * 2 + core
            landed(slot)

            @pl.when(j == 3)
            def _():
                for a in range(2):
                    kv_copy(a, 2).wait_send()
                for d in (1, 3, 2):
                    q_copy(d).start()

            for a in range(2):
                pass_on(a, slot, cross_send.at[a, j - 1], sibling).wait_send()
                pass_on(a, slot, cross_send.at[a, j], at(1, y, core)).start()
            pass_to_sibling(slot, j)
            turn(slot)
            return 0

        lax.fori_loop(1, 4, relay, 0)

        def from_sibling(j, _):
            slot = ((y + across(j)) % 4) * 2 + 1 - core
            landed(slot)
            turn(slot)
            return 0

        lax.fori_loop(0, 4, from_sibling, 0)

        def rows_of(j, _):
            d = along(j)
            n = (y + d) % 4

            @pl.when(j > 0)
            def _():
                q_landed(d)

            diagonal(n * 2 + core, n * 2 + 1 - core, n)

            @pl.when(n > 0)
            def _():
                def step(p, top_a):
                    return whole(p * 2 + core, p * 2 + 1 - core, n, jnp.minimum(p + 1, n - 1) * 2 + core, n, top_a)

                lax.fori_loop(0, n, step, put_score(core, n, 0))

            finish(n, 0)
            return 0

        lax.fori_loop(0, 4, rows_of, 0)

    @pl.when(half == 1)
    def _():
        def visited(v):
            j, kind = v // 2, v % 2
            d = (1 - kind) * along(j) + kind * across(j)
            return (y + d) % 4 + 4 * (1 - kind), kind

        def forward(v, _):
            slot = visited(v)[0] * 2 + core
            landed(slot)
            pass_to_sibling(slot, v)
            turn(slot)
            return 0

        turn(mine)
        for d in (1, 3, 2):
            q_copy(d).wait_send()
        for d in (1, 3):
            for a in range(2):
                kv_copy(a, d).start()
        forward(1, 0)
        for d in (1, 3, 2):
            q_landed(d)

        def visit(v, _):
            pair, kind = visited(v)
            slot_a, slot_b = pair * 2 + core, pair * 2 + 1 - core
            first = (pair - 4) * (1 - kind)
            count = kind * jnp.minimum(pair + 2, 4) + (1 - kind) * (3 - first)
            begin = (first + 1) * (1 - kind)
            final = v == 7

            @pl.when(final)
            def _():
                lax.fori_loop(count, 4, finish, 0)

            @pl.when(v == 2)
            def _():
                for d in (1, 3):
                    for a in range(2):
                        kv_copy(a, d).wait_send()
                for a in range(2):
                    kv_copy(a, 2).start()

            for at_visit, low, high in ((2, 2, 5), (5, 5, 7), (7, 7, 8)):
                @pl.when(v == at_visit)
                def _():
                    lax.fori_loop(low, high, forward, 0)

            landed(slot_b)
            turn(slot_b)

            @pl.when(kind == 0)
            def _():
                diagonal(slot_a, slot_b, first)

            @pl.when(count > 0)
            def _():
                def nth(i):
                    return begin + (i + kind * (y + 1)) % count

                def step(i, top_a):
                    n = nth(i)
                    top_a = whole(slot_a, slot_b, n, slot_a, nth(jnp.minimum(i + 1, count - 1)), top_a)

                    @pl.when(final)
                    def _():
                        finish(n, 0)
                    return top_a

                lax.fori_loop(0, count, step, put_score(slot_a, nth(0), 0))

            return 0

        lax.fori_loop(0, 8, visit, 0)

    own = pltpu.make_async_copy(obuf.at[y], rows_ref.at[:, head_columns(y)], own_sem.at[4])
    own.start()
    total = part[y]
    for d in (1, 3, 2):
        other = (y + d) % 4
        remote(part.at[y], parts.at[other], p_send.at[y], p_recv.at[other], sibling).wait_recv()
        total = total + parts[other]
    square[...] = total

    def s_copy(d):
        return remote(square, squares.at[tp], s_send.at[d], s_recv.at[16 - d], (mine, (tp + d) % 16))

    for d in range(1, 16):
        s_copy(d).start()
    for d in range(1, 16):
        other = (tp + d) % 16
        remote(square, squares.at[other], s_send.at[d], s_recv.at[d], sibling).wait_recv()
        total = total + squares[other]
    factor_ref[...] = lax.rsqrt(total * (1.0 / D) + EPSILON)

    own.wait()
    for d in (1, 3, 2):
        other = (y + d) % 4
        remote(obuf.at[y], rows_ref.at[:, head_columns(other)], o_send.at[y], o_recv.at[other], sibling).wait_recv()
        o_copy(other).wait_send()
        p_copy(other).wait_send()

        @pl.when(half == 0)
        def _():
            q_copy(d).wait_send()
    for d in range(1, 16):
        s_copy(d).wait_send()
        doc_copy(d).wait_send()

    def sent(v, _):
        for a in range(2):
            pass_on(a, mine, fwd_send.at[a, v], sibling).wait_send()
        return 0

    lax.fori_loop(0, 4 + 4 * half, sent, 0)

    @pl.when(half == 0)
    def _():
        for a in range(2):
            pass_on(a, mine, cross_send.at[a, 3], sibling).wait_send()

    @pl.when(half == 1)
    def _():
        for a in range(2):
            kv_copy(a, 2).wait_send()


def fused(queries, keys, values, docs):
    hbm = pl.BlockSpec(memory_space=pltpu.HBM)
    vmem = pl.BlockSpec(memory_space=pltpu.VMEM)
    dma = pltpu.SemaphoreType.DMA
    bf16, f32 = jnp.bfloat16, jnp.float32
    return pl.pallas_call(
        fused_kernel,
        name="fused",
        out_shape=[
            jax.ShapeDtypeStruct((CHUNK, 4 * HEAD_DIM), bf16),
            jax.ShapeDtypeStruct((1, CHUNK), f32),
        ],
        in_specs=[hbm] * 4,
        out_specs=[vmem] * 2,
        scratch_shapes=[
            pltpu.VMEM((4, CHUNK, HEAD_DIM), bf16),
            pltpu.VMEM((16, CHUNK, HEAD_DIM), bf16),
            pltpu.VMEM((16, CHUNK, HEAD_DIM), bf16),
            pltpu.VMEM((16, 4, 128), jnp.int32),
            pltpu.VMEM((4, CHUNK, HEAD_DIM), bf16),
            pltpu.VMEM((16, CHUNK, HEAD_DIM), bf16),
            pltpu.VMEM((16, ROWS, CHUNK), bf16),
            pltpu.VMEM((2, CHUNK, CHUNK), f32),
            pltpu.VMEM((4, ROWS, CHUNK), f32),
            pltpu.VMEM((4, 1, CHUNK), f32),
            pltpu.VMEM((4, CHUNK, HEAD_DIM), bf16),
            pltpu.VMEM((4, 1, CHUNK), f32),
            pltpu.VMEM((4, 1, CHUNK), f32),
            pltpu.VMEM((1, CHUNK), f32),
            pltpu.VMEM((16, 1, CHUNK), f32),
            dma((4,)), dma((4,)), dma((2, 4)), dma((2, 16)), dma((2, 8)), dma((2, 4)), dma((16,)), dma((16,)), dma((5,)),
            dma((4,)), dma((4,)), dma((4,)), dma((4,)), dma((16,)), dma((16,)),
        ],
        compiler_params=pltpu.CompilerParams(collective_id=0, has_side_effects=True, vmem_limit_bytes=62 * 10**6),
    )(queries, keys, values, docs)


def local(queries, keys, values, doc_ids, attn_gain):
    rows, factor = fused(queries, keys, values, doc_ids.reshape(4, 128))
    blended = attn_gain[None, :] * rows.astype(jnp.float32) * factor.reshape(CHUNK, 1)
    return blended.astype(jnp.bfloat16)


def solution(mesh):
    placed = (P("ctx", "tp"), P("ctx", "tp"), P("ctx", "tp"), P("ctx"), P("tp"))
    return jax.shard_map(
        local, mesh=mesh, in_specs=placed, out_specs=P("ctx", "tp"), check_vma=False
    )
```

```python
import math

import jax
import jax.numpy as jnp
from jax import lax
from jax.experimental import pallas as pl
from jax.experimental.pallas import tpu as pltpu
from jax.sharding import PartitionSpec as P

D = 8192
HEAD_DIM = 128
CHUNK = 512
REACH = 5
EPSILON = 1e-06
MASKED = -1e29
LOWEST = -1e20
OTHER_DOC = -(2.0**100)
SCALE = 1.4426950408889634 / math.sqrt(HEAD_DIM)
ROWS = HEAD_DIM + 16
MESH = pl.DeviceIdType.MESH


def head_columns(head):
    return pl.ds(pl.multiple_of(head * HEAD_DIM, HEAD_DIM), HEAD_DIM)


def fused_kernel(
    q_ref, k_ref, v_ref, doc_ref, rows_ref, factor_ref,
    qbuf, kbuf, vbuf, docs, qfeat, kfeat, vt, sbuf, acc, top, obuf, part, parts, square, squares,
    q_send, q_recv, kv_send, kv_recv, fwd_send, cross_send, doc_send, doc_recv, own_sem,
    o_send, o_recv, p_send, p_recv, s_send, s_recv,
):
    ctx, tp = lax.axis_index("ctx"), lax.axis_index("tp")
    half, y, core = ctx // 8, (ctx // 2) % 4, ctx % 2
    mine = half * 8 + y * 2 + core

    def at(h, yy, c):
        return (h * 8 + yy * 2 + c, tp)

    sibling = at(half, y, 1 - core)

    barrier = pltpu.get_barrier_semaphore()
    for d in range(1, 16):
        pl.semaphore_signal(barrier, inc=1, device_id=((mine + d) % 16, tp), device_id_type=MESH)
    for d in range(1, 16):
        pl.semaphore_signal(barrier, inc=1, device_id=(mine, (tp + d) % 16), device_id_type=MESH)
    pl.semaphore_wait(barrier, 30)

    kv = ((k_ref, kbuf), (v_ref, vbuf))

    def remote(src, dst, send, recv, device):
        return pltpu.make_async_remote_copy(src_ref=src, dst_ref=dst, send_sem=send, recv_sem=recv, device_id=device, device_id_type=MESH)

    def doc_copy(d):
        return remote(doc_ref, docs.at[mine], doc_send.at[d], doc_recv.at[16 - d], ((mine + d) % 16, tp))

    def q_copy(d):
        other = (y + d) % 4
        return remote(q_ref.at[:, head_columns(other)], qbuf.at[y], q_send.at[d], q_recv.at[4 - d], at(half, other, core))

    def kv_copy(a, d):
        other = (y + d) % 4
        return remote(kv[a][0].at[:, head_columns(other)], kv[a][1].at[mine], kv_send.at[a, d], kv_recv.at[a, mine], at(half, other, core))

    def own_copy(a, send, device):
        return remote(kv[a][0].at[:, head_columns(y)], kv[a][1].at[mine], send, kv_recv.at[a, mine], device)

    def pass_on(a, slot, send, device):
        return remote(kv[a][1].at[slot], kv[a][1].at[slot], send, kv_recv.at[a, slot], device)

    def landed(slot):
        for a in range(2):
            pass_on(a, slot, kv_send.at[a, 0], sibling).wait_recv()

    for d in range(1, 16):
        doc_copy(d).start()
    locals_ = [
        pltpu.make_async_copy(doc_ref, docs.at[mine], own_sem.at[0]),
        pltpu.make_async_copy(q_ref.at[:, head_columns(y)], qbuf.at[y], own_sem.at[1]),
        pltpu.make_async_copy(k_ref.at[:, head_columns(y)], kbuf.at[mine], own_sem.at[2]),
        pltpu.make_async_copy(v_ref.at[:, head_columns(y)], vbuf.at[mine], own_sem.at[3]),
    ]
    for c in locals_:
        c.start()

    @pl.when(half == 0)
    def _():
        for a in range(2):
            own_copy(a, cross_send.at[a, 0], at(1, y, core)).start()
        for d in (1, 3):
            for a in range(2):
                kv_copy(a, d).start()

    @pl.when(half == 1)
    def _():
        for d in (1, 3, 2):
            q_copy(d).start()

    for a in range(2):
        own_copy(a, fwd_send.at[a, 0], sibling).start()

    acc[...] = jnp.zeros(acc.shape, jnp.float32)
    top[...] = jnp.full(top.shape, LOWEST, jnp.float32)

    def ones_rows(n, _):
        vt[n, HEAD_DIM:, :] = jnp.ones((ROWS - HEAD_DIM, CHUNK), jnp.bfloat16)
        return 0

    lax.fori_loop(0, 8 + 8 * half, ones_rows, 0)

    for d in range(1, 16):
        remote(doc_ref, docs.at[mine], doc_send.at[d], doc_recv.at[d], sibling).wait_recv()
    for c in locals_:
        c.wait()

    def count(below):
        ones = jnp.where(docs[...] < below, 1.0, 0.0)
        return jnp.sum(jnp.sum(jnp.sum(ones, axis=0), axis=0, keepdims=True), axis=1, keepdims=True)

    second, third = count(1), count(2)
    lane = lax.broadcasted_iota(jnp.int32, (CHUNK, HEAD_DIM), 1)

    def doc_of(chunk):
        t = (chunk * CHUNK + lax.broadcasted_iota(jnp.int32, (CHUNK, HEAD_DIM), 0)).astype(jnp.float32)
        return jnp.where(t >= third, 2, jnp.where(t >= second, 1, 0))

    def key_features(s, _):
        kfeat[s] = jnp.where((lane < 3) & (lane != doc_of(s)), OTHER_DOC, 0.0).astype(jnp.bfloat16)
        return 0

    lax.fori_loop(0, half * 8 + 8, key_features, 0)

    def query_features(n, _):
        qfeat[n] = jnp.where(lane == doc_of(half * 8 + n * 2 + core), 1.0, 0.0).astype(jnp.bfloat16)
        return 0

    lax.fori_loop(0, 4, query_features, 0)

    def along(j):
        return j + j // 2 - 2 * (j // 3)

    falling = ((y + 1) // 2 + 1) % 2
    swapped = (y // 2) * (1 - falling)

    def across(j):
        return falling * ((4 - j) % 4) + (1 - falling) * (j + swapped * (j // 2) * (5 - 2 * j))

    def pass_to_sibling(slot, n):
        for a in range(2):
            pass_on(a, slot, fwd_send.at[a, n], sibling).start()

    def turn(slot):
        vt[slot, :HEAD_DIM, :] = vbuf[slot].T

    def q_landed(d):
        remote(qbuf.at[y], qbuf.at[y], q_send.at[0], q_recv.at[d], sibling).wait_recv()

    def score(slot, n):
        k = jnp.concatenate([kbuf[slot], kfeat[slot]], axis=1)
        q = jnp.concatenate([qbuf[n], qfeat[n]], axis=1)
        return lax.dot_general(k, q, (((1,), (1,)), ((), ())), preferred_element_type=jnp.float32) * SCALE

    def put_score(slot, n, buf):
        s = score(slot, n)
        sbuf[buf] = s
        return jnp.max(s, axis=0, keepdims=True)

    def absorb(state, s, s_top, slot):
        t, a = state
        new = jnp.maximum(t, s_top)
        p = jnp.exp2(s - new).astype(jnp.bfloat16)
        return new, a * jnp.exp2(t - new) + jnp.dot(vt[slot], p, preferred_element_type=jnp.float32)

    def diagonal(slot_a, slot_b, n):
        def masked():
            key = lax.broadcasted_iota(jnp.int32, (CHUNK, CHUNK), 0)
            query = lax.broadcasted_iota(jnp.int32, (CHUNK, CHUNK), 1)
            return jnp.where(key <= query, score(slot_a, n), MASKED)

        @pl.when(core == 0)
        def _():
            s = masked()
            t, a = absorb((top[n], acc[n]), s, jnp.max(s, axis=0, keepdims=True), slot_a)
            top[n] = t
            acc[n] = a

        @pl.when(core == 1)
        def _():
            s_b, s_a = score(slot_b, n), masked()
            t = top[n]
            new = jnp.maximum(t, jnp.maximum(jnp.max(s_a, axis=0, keepdims=True), jnp.max(s_b, axis=0, keepdims=True)))
            p_b = jnp.exp2(s_b - new).astype(jnp.bfloat16)
            p_a = jnp.exp2(s_a - new).astype(jnp.bfloat16)
            top[n] = new
            acc[n] = (
                acc[n] * jnp.exp2(t - new)
                + jnp.dot(vt[slot_b], p_b, preferred_element_type=jnp.float32)
                + jnp.dot(vt[slot_a], p_a, preferred_element_type=jnp.float32)
            )

    def whole(slot_a, slot_b, n, next_a, next_n, top_a):
        state = (top[n], acc[n])
        top_b = put_score(slot_b, n, 1)
        state = absorb(state, sbuf[0], top_a, slot_a)
        top_a = put_score(next_a, next_n, 0)
        t, a = absorb(state, sbuf[1], top_b, slot_b)
        top[n] = t
        acc[n] = a
        return top_a

    def o_copy(n):
        return remote(obuf.at[n], rows_ref.at[:, head_columns(y)], o_send.at[n], o_recv.at[y], at(half, n, core))

    def p_copy(n):
        return remote(part.at[n], parts.at[y], p_send.at[n], p_recv.at[y], at(half, n, core))

    def finish(n, _):
        a = acc[n]
        o = a[:HEAD_DIM] * (1.0 / a[HEAD_DIM:HEAD_DIM + 1])
        part[n] = jnp.sum(o * o, axis=0, keepdims=True)

        @pl.when(n != y)
        def _():
            p_copy(n).start()

        obuf[n] = o.T.astype(jnp.bfloat16)

        @pl.when(n != y)
        def _():
            o_copy(n).start()
        return 0

    @pl.when(half == 0)
    def _():
        turn(mine)
        for d in (1, 3):
            for a in range(2):
                kv_copy(a, d).wait_send()
        for a in range(2):
            kv_copy(a, 2).start()

        def relay(j, _):
            slot = ((y + across(j)) % 4) * 2 + core
            landed(slot)

            @pl.when(j == 3)
            def _():
                for a in range(2):
                    kv_copy(a, 2).wait_send()
                for d in (1, 3, 2):
                    q_copy(d).start()

            for a in range(2):
                pass_on(a, slot, cross_send.at[a, j - 1], sibling).wait_send()
                pass_on(a, slot, cross_send.at[a, j], at(1, y, core)).start()
            pass_to_sibling(slot, j)
            turn(slot)
            return 0

        lax.fori_loop(1, 4, relay, 0)

        def from_sibling(j, _):
            slot = ((y + across(j)) % 4) * 2 + 1 - core
            landed(slot)
            turn(slot)
            return 0

        lax.fori_loop(0, 4, from_sibling, 0)

        def rows_of(j, _):
            d = along(j)
            n = (y + d) % 4

            @pl.when(j > 0)
            def _():
                q_landed(d)

            diagonal(n * 2 + core, n * 2 + 1 - core, n)

            @pl.when(n > 0)
            def _():
                def step(p, top_a):
                    return whole(p * 2 + core, p * 2 + 1 - core, n, jnp.minimum(p + 1, n - 1) * 2 + core, n, top_a)

                lax.fori_loop(0, n, step, put_score(core, n, 0))

            finish(n, 0)
            return 0

        lax.fori_loop(0, 4, rows_of, 0)

    @pl.when(half == 1)
    def _():
        def visited(v):
            kind = jnp.where((v == 1) | (v == 4) | (v > 5), 1, 0)
            j = jnp.where(v < 2, 0, jnp.where((v == 2) | (v == 4), 1, jnp.where((v == 3) | (v == 6), 2, 3)))
            d = (1 - kind) * along(j) + kind * across(j)
            return (y + d) % 4 + 4 * (1 - kind), kind

        def forward(v, _):
            slot = visited(v)[0] * 2 + core
            landed(slot)
            pass_to_sibling(slot, v)
            turn(slot)
            return 0

        turn(mine)
        for d in (1, 3, 2):
            q_copy(d).wait_send()
        for d in (1, 3):
            for a in range(2):
                kv_copy(a, d).start()
        forward(1, 0)
        for d in (1, 3, 2):
            q_landed(d)

        def visit(v, _):
            pair, kind = visited(v)
            slot_a, slot_b = pair * 2 + core, pair * 2 + 1 - core
            first = (pair - 4) * (1 - kind)
            count = kind * jnp.minimum(pair + 2, 4) + (1 - kind) * (3 - first)
            begin = (first + 1) * (1 - kind)
            final = v == 7

            def ahead():
                for at_visit, low, high in ((1, 2, 4), (2, 4, 5), (4, 5, 6), (5, 6, 7), (6, 7, 8)):
                    @pl.when(v == at_visit)
                    def _():
                        lax.fori_loop(low, high, forward, 0)

            @pl.when(final)
            def _():
                lax.fori_loop(count, 4, finish, 0)

            @pl.when(v == 2)
            def _():
                for d in (1, 3):
                    for a in range(2):
                        kv_copy(a, d).wait_send()
                for a in range(2):
                    kv_copy(a, 2).start()

            landed(slot_b)
            turn(slot_b)

            pl.when(count == 0)(ahead)

            @pl.when(kind == 0)
            def _():
                diagonal(slot_a, slot_b, first)

            @pl.when(count > 0)
            def _():
                def nth(i):
                    return begin + (i + kind * (y + 1)) % count

                def step(i, top_a):
                    n = nth(i)
                    pl.when(i == count - 1)(ahead)
                    top_a = whole(slot_a, slot_b, n, slot_a, nth(jnp.minimum(i + 1, count - 1)), top_a)

                    @pl.when(final)
                    def _():
                        finish(n, 0)
                    return top_a

                lax.fori_loop(0, count, step, put_score(slot_a, nth(0), 0))

            return 0

        lax.fori_loop(0, 8, visit, 0)

    own = pltpu.make_async_copy(obuf.at[y], rows_ref.at[:, head_columns(y)], own_sem.at[4])
    own.start()
    total = part[y]
    for d in (1, 3, 2):
        other = (y + d) % 4
        remote(part.at[y], parts.at[other], p_send.at[y], p_recv.at[other], sibling).wait_recv()
        total = total + parts[other]
    square[...] = total

    def s_copy(d):
        return remote(square, squares.at[tp], s_send.at[d], s_recv.at[16 - d], (mine, (tp + d) % 16))

    for d in range(1, 16):
        s_copy(d).start()
    for d in range(1, 16):
        other = (tp + d) % 16
        remote(square, squares.at[other], s_send.at[d], s_recv.at[d], sibling).wait_recv()
        total = total + squares[other]
    factor_ref[...] = lax.rsqrt(total * (1.0 / D) + EPSILON)

    own.wait()
    for d in (1, 3, 2):
        other = (y + d) % 4
        remote(obuf.at[y], rows_ref.at[:, head_columns(other)], o_send.at[y], o_recv.at[other], sibling).wait_recv()
        o_copy(other).wait_send()
        p_copy(other).wait_send()

        @pl.when(half == 0)
        def _():
            q_copy(d).wait_send()
    for d in range(1, 16):
        s_copy(d).wait_send()
        doc_copy(d).wait_send()

    def sent(v, _):
        for a in range(2):
            pass_on(a, mine, fwd_send.at[a, v], sibling).wait_send()
        return 0

    lax.fori_loop(0, 4 + 4 * half, sent, 0)

    @pl.when(half == 0)
    def _():
        for a in range(2):
            pass_on(a, mine, cross_send.at[a, 3], sibling).wait_send()

    @pl.when(half == 1)
    def _():
        for a in range(2):
            kv_copy(a, 2).wait_send()


def fused(queries, keys, values, docs):
    hbm = pl.BlockSpec(memory_space=pltpu.HBM)
    vmem = pl.BlockSpec(memory_space=pltpu.VMEM)
    dma = pltpu.SemaphoreType.DMA
    bf16, f32 = jnp.bfloat16, jnp.float32
    return pl.pallas_call(
        fused_kernel,
        name="fused",
        out_shape=[
            jax.ShapeDtypeStruct((CHUNK, 4 * HEAD_DIM), bf16),
            jax.ShapeDtypeStruct((1, CHUNK), f32),
        ],
        in_specs=[hbm] * 4,
        out_specs=[vmem] * 2,
        scratch_shapes=[
            pltpu.VMEM((4, CHUNK, HEAD_DIM), bf16),
            pltpu.VMEM((16, CHUNK, HEAD_DIM), bf16),
            pltpu.VMEM((16, CHUNK, HEAD_DIM), bf16),
            pltpu.VMEM((16, 4, 128), jnp.int32),
            pltpu.VMEM((4, CHUNK, HEAD_DIM), bf16),
            pltpu.VMEM((16, CHUNK, HEAD_DIM), bf16),
            pltpu.VMEM((16, ROWS, CHUNK), bf16),
            pltpu.VMEM((2, CHUNK, CHUNK), f32),
            pltpu.VMEM((4, ROWS, CHUNK), f32),
            pltpu.VMEM((4, 1, CHUNK), f32),
            pltpu.VMEM((4, CHUNK, HEAD_DIM), bf16),
            pltpu.VMEM((4, 1, CHUNK), f32),
            pltpu.VMEM((4, 1, CHUNK), f32),
            pltpu.VMEM((1, CHUNK), f32),
            pltpu.VMEM((16, 1, CHUNK), f32),
            dma((4,)), dma((4,)), dma((2, 4)), dma((2, 16)), dma((2, 8)), dma((2, 4)), dma((16,)), dma((16,)), dma((5,)),
            dma((4,)), dma((4,)), dma((4,)), dma((4,)), dma((16,)), dma((16,)),
        ],
        compiler_params=pltpu.CompilerParams(collective_id=0, has_side_effects=True, vmem_limit_bytes=56 * 10**6),
    )(queries, keys, values, docs)


def local(queries, keys, values, doc_ids, attn_gain):
    rows, factor = fused(queries, keys, values, doc_ids.reshape(4, 128))
    blended = attn_gain[None, :] * rows.astype(jnp.float32) * factor.reshape(CHUNK, 1)
    return blended.astype(jnp.bfloat16)


def solution(mesh):
    placed = (P("ctx", "tp"), P("ctx", "tp"), P("ctx", "tp"), P("ctx"), P("tp"))
    return jax.shard_map(
        local, mesh=mesh, in_specs=placed, out_specs=P("ctx", "tp"), check_vma=False
    )
```

```python
import math

import jax
import jax.numpy as jnp
from jax import lax
from jax.experimental import pallas as pl
from jax.experimental.pallas import tpu as pltpu
from jax.sharding import PartitionSpec as P

D = 8192
HEAD_DIM = 128
CHUNK = 512
REACH = 5
EPSILON = 1e-06
MASKED = -1e29
LOWEST = -1e20
OTHER_DOC = -(2.0**100)
SCALE = 1.4426950408889634 / math.sqrt(HEAD_DIM)
ROWS = HEAD_DIM + 16
MESH = pl.DeviceIdType.MESH


def head_columns(head):
    return pl.ds(pl.multiple_of(head * HEAD_DIM, HEAD_DIM), HEAD_DIM)


def fused_kernel(
    q_ref, k_ref, v_ref, doc_ref, gain_ref, rows_ref, factor_ref,
    gain, qbuf, kbuf, vbuf, docs, qfeat, kfeat, vt, sbuf, acc, top, obuf, part, parts, square, squares,
    q_send, q_recv, kv_send, kv_recv, fwd_send, cross_send, doc_send, doc_recv, own_sem,
    o_send, o_recv, p_send, p_recv, s_send, s_recv,
):
    ctx, tp = lax.axis_index("ctx"), lax.axis_index("tp")
    half, y, core = ctx // 8, (ctx // 2) % 4, ctx % 2
    mine = half * 8 + y * 2 + core

    def at(h, yy, c):
        return (h * 8 + yy * 2 + c, tp)

    sibling = at(half, y, 1 - core)

    barrier = pltpu.get_barrier_semaphore()
    for d in range(1, 16):
        pl.semaphore_signal(barrier, inc=1, device_id=((mine + d) % 16, tp), device_id_type=MESH)
    for d in range(1, 16):
        pl.semaphore_signal(barrier, inc=1, device_id=(mine, (tp + d) % 16), device_id_type=MESH)
    pl.semaphore_wait(barrier, 30)

    kv = ((k_ref, kbuf), (v_ref, vbuf))

    def remote(src, dst, send, recv, device):
        return pltpu.make_async_remote_copy(src_ref=src, dst_ref=dst, send_sem=send, recv_sem=recv, device_id=device, device_id_type=MESH)

    def doc_copy(d):
        return remote(doc_ref, docs.at[mine], doc_send.at[d], doc_recv.at[16 - d], ((mine + d) % 16, tp))

    def q_copy(d):
        other = (y + d) % 4
        return remote(q_ref.at[:, head_columns(other)], qbuf.at[y], q_send.at[d], q_recv.at[4 - d], at(half, other, core))

    def kv_copy(a, d):
        other = (y + d) % 4
        return remote(kv[a][0].at[:, head_columns(other)], kv[a][1].at[mine], kv_send.at[a, d], kv_recv.at[a, mine], at(half, other, core))

    def own_copy(a, send, device):
        return remote(kv[a][0].at[:, head_columns(y)], kv[a][1].at[mine], send, kv_recv.at[a, mine], device)

    def pass_on(a, slot, send, device):
        return remote(kv[a][1].at[slot], kv[a][1].at[slot], send, kv_recv.at[a, slot], device)

    def landed(slot):
        for a in range(2):
            pass_on(a, slot, kv_send.at[a, 0], sibling).wait_recv()

    for d in range(1, 16):
        doc_copy(d).start()
    locals_ = [
        pltpu.make_async_copy(doc_ref, docs.at[mine], own_sem.at[0]),
        pltpu.make_async_copy(q_ref.at[:, head_columns(y)], qbuf.at[y], own_sem.at[1]),
        pltpu.make_async_copy(gain_ref.at[:, head_columns(y)], gain, own_sem.at[5]),
        pltpu.make_async_copy(k_ref.at[:, head_columns(y)], kbuf.at[mine], own_sem.at[2]),
        pltpu.make_async_copy(v_ref.at[:, head_columns(y)], vbuf.at[mine], own_sem.at[3]),
    ]
    for c in locals_:
        c.start()

    @pl.when(half == 0)
    def _():
        for a in range(2):
            for d in (1, 3):
                kv_copy(a, d).start()
            own_copy(a, cross_send.at[a, 0], at(1, y, core)).start()

    @pl.when(half == 1)
    def _():
        for d in (1, 3, 2):
            q_copy(d).start()

    @pl.when(half == 1)
    def _():
        for a in range(2):
            own_copy(a, fwd_send.at[a, 0], sibling).start()

    acc[...] = jnp.zeros(acc.shape, jnp.float32)
    top[...] = jnp.full(top.shape, LOWEST, jnp.float32)

    def ones_rows(n, _):
        vt[n, HEAD_DIM:, :] = jnp.ones((ROWS - HEAD_DIM, CHUNK), jnp.bfloat16)
        return 0

    lax.fori_loop(0, 8 + 8 * half, ones_rows, 0)

    for d in range(1, 16):
        remote(doc_ref, docs.at[mine], doc_send.at[d], doc_recv.at[d], sibling).wait_recv()
    for c in locals_:
        c.wait()

    def count(below):
        ones = jnp.where(docs[...] < below, 1.0, 0.0)
        return jnp.sum(jnp.sum(jnp.sum(ones, axis=0), axis=0, keepdims=True), axis=1, keepdims=True)

    second, third = count(1), count(2)
    lane = lax.broadcasted_iota(jnp.int32, (CHUNK, HEAD_DIM), 1)

    def doc_of(chunk):
        t = (chunk * CHUNK + lax.broadcasted_iota(jnp.int32, (CHUNK, HEAD_DIM), 0)).astype(jnp.float32)
        return jnp.where(t >= third, 2, jnp.where(t >= second, 1, 0))

    def key_features(s, _):
        kfeat[s] = jnp.where((lane < 3) & (lane != doc_of(s)), OTHER_DOC, 0.0).astype(jnp.bfloat16)
        return 0

    lax.fori_loop(0, half * 8 + 8, key_features, 0)

    def query_features(n, _):
        qfeat[n] = jnp.where(lane == doc_of(half * 8 + n * 2 + core), 1.0, 0.0).astype(jnp.bfloat16)
        return 0

    lax.fori_loop(0, 4, query_features, 0)

    def along(j):
        return j + j // 2 - 2 * (j // 3)

    falling = ((y + 1) // 2 + 1) % 2
    swapped = (y // 2) * (1 - falling)

    def across(j):
        return falling * ((4 - j) % 4) + (1 - falling) * (j + swapped * (j // 2) * (5 - 2 * j))

    def pass_to_sibling(slot, n):
        for a in range(2):
            pass_on(a, slot, fwd_send.at[a, n], sibling).start()

    def turn(slot):
        vt[slot, :HEAD_DIM, :] = vbuf[slot].T

    def q_landed(d):
        remote(qbuf.at[y], qbuf.at[y], q_send.at[0], q_recv.at[d], sibling).wait_recv()

    def score(slot, n):
        k = jnp.concatenate([kbuf[slot], kfeat[slot]], axis=1)
        q = jnp.concatenate([qbuf[n], qfeat[n]], axis=1)
        return lax.dot_general(k, q, (((1,), (1,)), ((), ())), preferred_element_type=jnp.float32) * SCALE

    def put_score(slot, n, buf):
        s = score(slot, n)
        sbuf[buf] = s
        return jnp.max(s, axis=0, keepdims=True)

    def absorb(state, s, s_top, slot):
        t, a = state
        new = jnp.maximum(t, s_top)
        p = jnp.exp2(s - new).astype(jnp.bfloat16)
        return new, a * jnp.exp2(t - new) + jnp.dot(vt[slot], p, preferred_element_type=jnp.float32)

    def diagonal(slot_a, slot_b, n):
        def masked():
            key = lax.broadcasted_iota(jnp.int32, (CHUNK, CHUNK), 0)
            query = lax.broadcasted_iota(jnp.int32, (CHUNK, CHUNK), 1)
            return jnp.where(key <= query, score(slot_a, n), MASKED)

        @pl.when(core == 0)
        def _():
            s = masked()
            t, a = absorb((top[n], acc[n]), s, jnp.max(s, axis=0, keepdims=True), slot_a)
            top[n] = t
            acc[n] = a

        @pl.when(core == 1)
        def _():
            s_b, s_a = score(slot_b, n), masked()
            t = top[n]
            new = jnp.maximum(t, jnp.maximum(jnp.max(s_a, axis=0, keepdims=True), jnp.max(s_b, axis=0, keepdims=True)))
            p_b = jnp.exp2(s_b - new).astype(jnp.bfloat16)
            p_a = jnp.exp2(s_a - new).astype(jnp.bfloat16)
            top[n] = new
            acc[n] = (
                acc[n] * jnp.exp2(t - new)
                + jnp.dot(vt[slot_b], p_b, preferred_element_type=jnp.float32)
                + jnp.dot(vt[slot_a], p_a, preferred_element_type=jnp.float32)
            )

    def whole(slot_a, slot_b, n, next_a, next_n, top_a):
        state = (top[n], acc[n])
        top_b = put_score(slot_b, n, 1)
        state = absorb(state, sbuf[0], top_a, slot_a)
        top_a = put_score(next_a, next_n, 0)
        t, a = absorb(state, sbuf[1], top_b, slot_b)
        top[n] = t
        acc[n] = a
        return top_a

    def o_copy(n):
        return remote(obuf.at[n], rows_ref.at[:, head_columns(y)], o_send.at[n], o_recv.at[y], at(half, n, core))

    def p_copy(n):
        return remote(part.at[n], parts.at[y], p_send.at[n], p_recv.at[y], at(half, n, core))

    def finish(n, _):
        a = acc[n]
        o = a[:HEAD_DIM] * (1.0 / a[HEAD_DIM:HEAD_DIM + 1])
        part[n] = jnp.sum(o * o, axis=0, keepdims=True)

        @pl.when(n != y)
        def _():
            p_copy(n).start()

        obuf[n] = (o.T * gain[...]).astype(jnp.bfloat16)

        @pl.when(n != y)
        def _():
            o_copy(n).start()
        return 0

    @pl.when(half == 0)
    def _():
        turn(mine)
        for d in (1, 3):
            for a in range(2):
                kv_copy(a, d).wait_send()
        for a in range(2):
            kv_copy(a, 2).start()

        def relay(j, _):
            slot = ((y + across(j)) % 4) * 2 + core
            landed(slot)

            @pl.when(j == 3)
            def _():
                for a in range(2):
                    kv_copy(a, 2).wait_send()
                for d in (1, 3, 2):
                    q_copy(d).start()

            for a in range(2):
                pass_on(a, slot, cross_send.at[a, j - 1], sibling).wait_send()
                pass_on(a, slot, cross_send.at[a, j], at(1, y, core)).start()
            pass_to_sibling(slot, j)
            turn(slot)
            return 0

        lax.fori_loop(1, 4, relay, 0)
        for a in range(2):
            own_copy(a, fwd_send.at[a, 0], sibling).start()

        def from_sibling(j, _):
            slot = ((y + across(j)) % 4) * 2 + 1 - core
            landed(slot)
            turn(slot)
            return 0

        lax.fori_loop(0, 4, from_sibling, 0)

        def rows_of(j, _):
            d = along(j)
            n = (y + d) % 4

            @pl.when(j > 0)
            def _():
                q_landed(d)

            diagonal(n * 2 + core, n * 2 + 1 - core, n)

            @pl.when(n > 0)
            def _():
                def step(p, top_a):
                    return whole(p * 2 + core, p * 2 + 1 - core, n, jnp.minimum(p + 1, n - 1) * 2 + core, n, top_a)

                lax.fori_loop(0, n, step, put_score(core, n, 0))

            finish(n, 0)
            return 0

        lax.fori_loop(0, 4, rows_of, 0)

    @pl.when(half == 1)
    def _():
        def visited(v):
            kind = jnp.where((v == 1) | (v == 4) | (v > 5), 1, 0)
            j = jnp.where(v < 2, 0, jnp.where((v == 2) | (v == 4), 1, jnp.where((v == 3) | (v == 6), 2, 3)))
            d = (1 - kind) * along(j) + kind * across(j)
            return (y + d) % 4 + 4 * (1 - kind), kind

        def forward(v, _):
            slot = visited(v)[0] * 2 + core
            landed(slot)
            pass_to_sibling(slot, v)
            turn(slot)
            return 0

        turn(mine)
        for d in (1, 3, 2):
            q_copy(d).wait_send()
        for a in range(2):
            for d in (1, 3):
                kv_copy(a, d).start()
        forward(1, 0)
        for d in (1, 3, 2):
            q_landed(d)

        def visit(v, _):
            pair, kind = visited(v)
            slot_a, slot_b = pair * 2 + core, pair * 2 + 1 - core
            first = (pair - 4) * (1 - kind)
            count = kind * jnp.minimum(pair + 2, 4) + (1 - kind) * (3 - first)
            begin = (first + 1) * (1 - kind)
            final = v == 7

            def ahead():
                for at_visit, low, high in ((1, 2, 4), (2, 4, 5), (4, 5, 6), (5, 6, 7), (6, 7, 8)):
                    @pl.when(v == at_visit)
                    def _():
                        lax.fori_loop(low, high, forward, 0)

            @pl.when(final)
            def _():
                lax.fori_loop(count, 4, finish, 0)

            @pl.when(v == 2)
            def _():
                for d in (1, 3):
                    for a in range(2):
                        kv_copy(a, d).wait_send()
                for a in range(2):
                    kv_copy(a, 2).start()

            landed(slot_b)
            turn(slot_b)

            pl.when(count == 0)(ahead)

            @pl.when(kind == 0)
            def _():
                diagonal(slot_a, slot_b, first)

            @pl.when(count > 0)
            def _():
                def nth(i):
                    return begin + (i + kind * (y + 1)) % count

                def step(i, top_a):
                    n = nth(i)
                    pl.when(i == count - 1)(ahead)
                    top_a = whole(slot_a, slot_b, n, slot_a, nth(jnp.minimum(i + 1, count - 1)), top_a)

                    @pl.when(final)
                    def _():
                        finish(n, 0)
                    return top_a

                lax.fori_loop(0, count, step, put_score(slot_a, nth(0), 0))

            return 0

        lax.fori_loop(0, 8, visit, 0)

    own = pltpu.make_async_copy(obuf.at[y], rows_ref.at[:, head_columns(y)], own_sem.at[4])
    own.start()
    total = part[y]
    for d in (1, 3, 2):
        other = (y + d) % 4
        remote(part.at[y], parts.at[other], p_send.at[y], p_recv.at[other], sibling).wait_recv()
        total = total + parts[other]
    square[...] = total

    def s_copy(d):
        return remote(square, squares.at[15 - d], s_send.at[0], s_recv.at[0], (mine, (tp + d) % 16))

    for d in range(1, 16):
        s_copy(d).start()
    all_sums = remote(squares, squares, s_send.at[0], s_recv.at[0], sibling)
    all_sums.wait_recv()
    total = total + jnp.sum(squares[...], axis=0)
    factor_ref[...] = lax.rsqrt(total * (1.0 / D) + EPSILON)

    own.wait()
    for d in (1, 3, 2):
        other = (y + d) % 4
        remote(obuf.at[y], rows_ref.at[:, head_columns(other)], o_send.at[y], o_recv.at[other], sibling).wait_recv()
        o_copy(other).wait_send()
        p_copy(other).wait_send()

        @pl.when(half == 0)
        def _():
            q_copy(d).wait_send()
    for d in range(1, 16):
        doc_copy(d).wait_send()

    all_sums.wait_send()

    def sent(v, _):
        for a in range(2):
            pass_on(a, mine, fwd_send.at[a, v], sibling).wait_send()
        return 0

    lax.fori_loop(0, 4 + 4 * half, sent, 0)

    @pl.when(half == 0)
    def _():
        for a in range(2):
            pass_on(a, mine, cross_send.at[a, 3], sibling).wait_send()

    @pl.when(half == 1)
    def _():
        for a in range(2):
            kv_copy(a, 2).wait_send()


def fused(queries, keys, values, docs, gain):
    hbm = pl.BlockSpec(memory_space=pltpu.HBM)
    vmem = pl.BlockSpec(memory_space=pltpu.VMEM)
    dma = pltpu.SemaphoreType.DMA
    bf16, f32 = jnp.bfloat16, jnp.float32
    return pl.pallas_call(
        fused_kernel,
        name="fused",
        out_shape=[
            jax.ShapeDtypeStruct((CHUNK, 4 * HEAD_DIM), bf16),
            jax.ShapeDtypeStruct((1, CHUNK), f32),
        ],
        in_specs=[hbm] * 5,
        out_specs=[vmem] * 2,
        scratch_shapes=[
            pltpu.VMEM((1, HEAD_DIM), f32),
            pltpu.VMEM((4, CHUNK, HEAD_DIM), bf16),
            pltpu.VMEM((16, CHUNK, HEAD_DIM), bf16),
            pltpu.VMEM((16, CHUNK, HEAD_DIM), bf16),
            pltpu.VMEM((16, 4, 128), jnp.int32),
            pltpu.VMEM((4, CHUNK, HEAD_DIM), bf16),
            pltpu.VMEM((16, CHUNK, HEAD_DIM), bf16),
            pltpu.VMEM((16, ROWS, CHUNK), bf16),
            pltpu.VMEM((2, CHUNK, CHUNK), f32),
            pltpu.VMEM((4, ROWS, CHUNK), f32),
            pltpu.VMEM((4, 1, CHUNK), f32),
            pltpu.VMEM((4, CHUNK, HEAD_DIM), bf16),
            pltpu.VMEM((4, 1, CHUNK), f32),
            pltpu.VMEM((4, 1, CHUNK), f32),
            pltpu.VMEM((1, CHUNK), f32),
            pltpu.VMEM((15, 1, CHUNK), f32),
            dma((4,)), dma((4,)), dma((2, 4)), dma((2, 16)), dma((2, 8)), dma((2, 4)), dma((16,)), dma((16,)), dma((6,)),
            dma((4,)), dma((4,)), dma((4,)), dma((4,)), dma((16,)), dma((16,)),
        ],
        compiler_params=pltpu.CompilerParams(collective_id=0, has_side_effects=True, vmem_limit_bytes=56 * 10**6),
    )(queries, keys, values, docs, gain)


def local(queries, keys, values, doc_ids, attn_gain):
    docs, gain = doc_ids.reshape(4, 128), attn_gain.reshape(1, 4 * HEAD_DIM)
    docs, gain = (pltpu.with_memory_space_constraint(x, pltpu.HBM) for x in (docs, gain))
    rows, factor = fused(queries, keys, values, docs, gain)
    return (rows.astype(jnp.float32) * factor.reshape(CHUNK, 1)).astype(jnp.bfloat16)


def solution(mesh):
    placed = (P("ctx", "tp"), P("ctx", "tp"), P("ctx", "tp"), P("ctx"), P("tp"))
    return jax.shard_map(
        local, mesh=mesh, in_specs=placed, out_specs=P("ctx", "tp"), check_vma=False
    )
```

```python
import math

import jax
import jax.numpy as jnp
from jax import lax
from jax.experimental import pallas as pl
from jax.experimental.pallas import tpu as pltpu
from jax.sharding import PartitionSpec as P

D = 8192
HEAD_DIM = 128
CHUNK = 512
REACH = 5
EPSILON = 1e-06
MASKED = -1e29
LOWEST = -1e20
OTHER_DOC = -(2.0**100)
SCALE = 1.4426950408889634 / math.sqrt(HEAD_DIM)
ROWS = HEAD_DIM + 16
MESH = pl.DeviceIdType.MESH


def head_columns(head):
    return pl.ds(pl.multiple_of(head * HEAD_DIM, HEAD_DIM), HEAD_DIM)


def fused_kernel(
    q_ref, k_ref, v_ref, doc_ref, gain_ref, rows_ref, factor_ref,
    gain, qbuf, kbuf, vbuf, docs, qfeat, kfeat, vt, sbuf, acc, top, obuf, part, parts, square, squares,
    q_send, q_recv, kv_send, kv_recv, fwd_send, cross_send, doc_send, doc_recv, own_sem,
    o_send, o_recv, p_send, p_recv, s_send, s_recv,
):
    ctx, tp = lax.axis_index("ctx"), lax.axis_index("tp")
    half, y, core = ctx // 8, (ctx // 2) % 4, ctx % 2
    mine = half * 8 + y * 2 + core

    def at(h, yy, c):
        return (h * 8 + yy * 2 + c, tp)

    sibling = at(half, y, 1 - core)

    barrier = pltpu.get_barrier_semaphore()
    for d in range(1, 16):
        pl.semaphore_signal(barrier, inc=1, device_id=((mine + d) % 16, tp), device_id_type=MESH)
    for d in range(1, 16):
        pl.semaphore_signal(barrier, inc=1, device_id=(mine, (tp + d) % 16), device_id_type=MESH)
    pl.semaphore_wait(barrier, 30)

    kv = ((k_ref, kbuf), (v_ref, vbuf))

    def remote(src, dst, send, recv, device):
        return pltpu.make_async_remote_copy(src_ref=src, dst_ref=dst, send_sem=send, recv_sem=recv, device_id=device, device_id_type=MESH)

    def doc_copy(d):
        return remote(doc_ref, docs.at[mine], doc_send.at[d], doc_recv.at[16 - d], ((mine + d) % 16, tp))

    def q_copy(d):
        other = (y + d) % 4
        return remote(q_ref.at[:, head_columns(other)], qbuf.at[y], q_send.at[d], q_recv.at[4 - d], at(half, other, core))

    def kv_copy(a, d):
        other = (y + d) % 4
        return remote(kv[a][0].at[:, head_columns(other)], kv[a][1].at[mine], kv_send.at[a, d], kv_recv.at[a, mine], at(half, other, core))

    def own_copy(a, send, device):
        return remote(kv[a][0].at[:, head_columns(y)], kv[a][1].at[mine], send, kv_recv.at[a, mine], device)

    def pass_on(a, slot, send, device):
        return remote(kv[a][1].at[slot], kv[a][1].at[slot], send, kv_recv.at[a, slot], device)

    def landed(slot):
        for a in range(2):
            pass_on(a, slot, kv_send.at[a, 0], sibling).wait_recv()

    for d in range(1, 16):
        doc_copy(d).start()
    locals_ = [
        pltpu.make_async_copy(doc_ref, docs.at[mine], own_sem.at[0]),
        pltpu.make_async_copy(q_ref.at[:, head_columns(y)], qbuf.at[y], own_sem.at[1]),
        pltpu.make_async_copy(gain_ref.at[:, head_columns(y)], gain, own_sem.at[5]),
        pltpu.make_async_copy(k_ref.at[:, head_columns(y)], kbuf.at[mine], own_sem.at[2]),
        pltpu.make_async_copy(v_ref.at[:, head_columns(y)], vbuf.at[mine], own_sem.at[3]),
    ]
    for c in locals_:
        c.start()

    @pl.when(half == 0)
    def _():
        for a in range(2):
            for d in (1, 3):
                kv_copy(a, d).start()
            own_copy(a, cross_send.at[a, 0], at(1, y, core)).start()

    @pl.when(half == 1)
    def _():
        for d in (1, 3, 2):
            q_copy(d).start()

    @pl.when(half == 1)
    def _():
        for a in range(2):
            own_copy(a, fwd_send.at[a, 0], sibling).start()

    acc[...] = jnp.zeros(acc.shape, jnp.float32)
    top[...] = jnp.full(top.shape, LOWEST, jnp.float32)

    def ones_rows(n, _):
        vt[n, HEAD_DIM:, :] = jnp.ones((ROWS - HEAD_DIM, CHUNK), jnp.bfloat16)
        return 0

    lax.fori_loop(0, 8 + 8 * half, ones_rows, 0)

    for d in range(1, 16):
        remote(doc_ref, docs.at[mine], doc_send.at[d], doc_recv.at[d], sibling).wait_recv()
    for c in locals_:
        c.wait()

    def count(below):
        ones = jnp.where(docs[...] < below, 1.0, 0.0)
        return jnp.sum(jnp.sum(jnp.sum(ones, axis=0), axis=0, keepdims=True), axis=1, keepdims=True)

    second, third = count(1), count(2)
    lane = lax.broadcasted_iota(jnp.int32, (CHUNK, HEAD_DIM), 1)

    def doc_of(chunk):
        t = (chunk * CHUNK + lax.broadcasted_iota(jnp.int32, (CHUNK, HEAD_DIM), 0)).astype(jnp.float32)
        return jnp.where(t >= third, 2, jnp.where(t >= second, 1, 0))

    def key_features(s, _):
        kfeat[s] = jnp.where((lane < 3) & (lane != doc_of(s)), OTHER_DOC, 0.0).astype(jnp.bfloat16)
        return 0

    lax.fori_loop(0, half * 8 + 8, key_features, 0)

    def query_features(n, _):
        qfeat[n] = jnp.where(lane == doc_of(half * 8 + n * 2 + core), 1.0, 0.0).astype(jnp.bfloat16)
        return 0

    lax.fori_loop(0, 4, query_features, 0)

    def along(j):
        return j + j // 2 - 2 * (j // 3)

    falling = ((y + 1) // 2 + 1) % 2
    swapped = (y // 2) * (1 - falling)

    def across(j):
        return falling * ((4 - j) % 4) + (1 - falling) * (j + swapped * (j // 2) * (5 - 2 * j))

    def pass_to_sibling(slot, n):
        for a in range(2):
            pass_on(a, slot, fwd_send.at[a, n], sibling).start()

    def turn(slot):
        vt[slot, :HEAD_DIM, :] = vbuf[slot].T

    def q_landed(d):
        remote(qbuf.at[y], qbuf.at[y], q_send.at[0], q_recv.at[d], sibling).wait_recv()

    def score(slot, n):
        k = jnp.concatenate([kbuf[slot], kfeat[slot]], axis=1)
        q = jnp.concatenate([qbuf[n], qfeat[n]], axis=1)
        return lax.dot_general(k, q, (((1,), (1,)), ((), ())), preferred_element_type=jnp.float32) * SCALE

    def put_score(slot, n, buf):
        s = score(slot, n)
        sbuf[buf] = s
        return jnp.max(s, axis=0, keepdims=True)

    def absorb(state, s, s_top, slot):
        t, a = state
        new = jnp.maximum(t, s_top)
        p = jnp.exp2(s - new).astype(jnp.bfloat16)
        return new, a * jnp.exp2(t - new) + jnp.dot(vt[slot], p, preferred_element_type=jnp.float32)

    def diagonal(slot_a, slot_b, n):
        def masked():
            key = lax.broadcasted_iota(jnp.int32, (CHUNK, CHUNK), 0)
            query = lax.broadcasted_iota(jnp.int32, (CHUNK, CHUNK), 1)
            return jnp.where(key <= query, score(slot_a, n), MASKED)

        @pl.when(core == 0)
        def _():
            s = masked()
            t, a = absorb((top[n], acc[n]), s, jnp.max(s, axis=0, keepdims=True), slot_a)
            top[n] = t
            acc[n] = a

        @pl.when(core == 1)
        def _():
            s_b, s_a = score(slot_b, n), masked()
            t = top[n]
            new = jnp.maximum(t, jnp.maximum(jnp.max(s_a, axis=0, keepdims=True), jnp.max(s_b, axis=0, keepdims=True)))
            p_b = jnp.exp2(s_b - new).astype(jnp.bfloat16)
            p_a = jnp.exp2(s_a - new).astype(jnp.bfloat16)
            top[n] = new
            acc[n] = (
                acc[n] * jnp.exp2(t - new)
                + jnp.dot(vt[slot_b], p_b, preferred_element_type=jnp.float32)
                + jnp.dot(vt[slot_a], p_a, preferred_element_type=jnp.float32)
            )

    def whole(slot_a, slot_b, n, next_a, next_n, top_a):
        state = (top[n], acc[n])
        top_b = put_score(slot_b, n, 1)
        state = absorb(state, sbuf[0], top_a, slot_a)
        top_a = put_score(next_a, next_n, 0)
        t, a = absorb(state, sbuf[1], top_b, slot_b)
        top[n] = t
        acc[n] = a
        return top_a

    def o_copy(n):
        return remote(obuf.at[n], rows_ref.at[:, head_columns(y)], o_send.at[n], o_recv.at[y], at(half, n, core))

    def p_copy(n):
        return remote(part.at[n], parts.at[y], p_send.at[n], p_recv.at[y], at(half, n, core))

    def finish(n, _):
        a = acc[n]
        o = a[:HEAD_DIM] * (1.0 / a[HEAD_DIM:HEAD_DIM + 1])
        part[n] = jnp.sum(o * o, axis=0, keepdims=True)

        @pl.when(n != y)
        def _():
            p_copy(n).start()

        obuf[n] = (o.T * gain[...]).astype(jnp.bfloat16)

        @pl.when(n != y)
        def _():
            o_copy(n).start()
        return 0

    @pl.when(half == 0)
    def _():
        turn(mine)
        for d in (1, 3):
            for a in range(2):
                kv_copy(a, d).wait_send()
        for a in range(2):
            kv_copy(a, 2).start()

        def relay(j, _):
            slot = ((y + across(j)) % 4) * 2 + core
            landed(slot)

            @pl.when(j == 3)
            def _():
                for a in range(2):
                    kv_copy(a, 2).wait_send()
                for d in (1, 3, 2):
                    q_copy(d).start()

            for a in range(2):
                pass_on(a, slot, cross_send.at[a, j - 1], sibling).wait_send()
                pass_on(a, slot, cross_send.at[a, j], at(1, y, core)).start()
            pass_to_sibling(slot, j)
            turn(slot)
            return 0

        lax.fori_loop(1, 4, relay, 0)
        for a in range(2):
            own_copy(a, fwd_send.at[a, 0], sibling).start()

        def from_sibling(j, _):
            slot = ((y + across(j)) % 4) * 2 + 1 - core
            landed(slot)
            turn(slot)
            return 0

        lax.fori_loop(0, 4, from_sibling, 0)

        def rows_of(j, _):
            d = along(j)
            n = (y + d) % 4

            @pl.when(j > 0)
            def _():
                q_landed(d)

            diagonal(n * 2 + core, n * 2 + 1 - core, n)

            @pl.when(n > 0)
            def _():
                def step(p, top_a):
                    return whole(p * 2 + core, p * 2 + 1 - core, n, jnp.minimum(p + 1, n - 1) * 2 + core, n, top_a)

                lax.fori_loop(0, n, step, put_score(core, n, 0))

            finish(n, 0)
            return 0

        lax.fori_loop(0, 4, rows_of, 0)

    @pl.when(half == 1)
    def _():
        def visited(v):
            kind = jnp.where((v == 1) | (v == 4) | (v > 5), 1, 0)
            j = jnp.where(v < 2, 0, jnp.where((v == 2) | (v == 4), 1, jnp.where((v == 3) | (v == 6), 2, 3)))
            d = (1 - kind) * along(j) + kind * across(j)
            return (y + d) % 4 + 4 * (1 - kind), kind

        def forward(v, _):
            slot = visited(v)[0] * 2 + core
            landed(slot)
            pass_to_sibling(slot, v)
            turn(slot)
            return 0

        turn(mine)
        for d in (1, 3, 2):
            q_copy(d).wait_send()
        for a in range(2):
            for d in (1, 3):
                kv_copy(a, d).start()
        forward(1, 0)
        for d in (1, 3, 2):
            q_landed(d)

        def visit(v, _):
            pair, kind = visited(v)
            slot_a, slot_b = pair * 2 + core, pair * 2 + 1 - core
            first = (pair - 4) * (1 - kind)
            count = kind * jnp.minimum(pair + 2, 4) + (1 - kind) * (3 - first)
            begin = (first + 1) * (1 - kind)
            final = v == 7

            def ahead():
                @pl.when(v == 1)
                def _():
                    for d in (1, 3):
                        for a in range(2):
                            kv_copy(a, d).wait_send()
                    for a in range(2):
                        kv_copy(a, 2).start()

                for at_visit, low, high in ((1, 2, 4), (2, 4, 5), (4, 5, 6), (5, 6, 7), (6, 7, 8)):
                    @pl.when(v == at_visit)
                    def _():
                        lax.fori_loop(low, high, forward, 0)

            @pl.when(final)
            def _():
                lax.fori_loop(count, 4, finish, 0)

            landed(slot_b)
            turn(slot_b)

            pl.when(count == 0)(ahead)

            @pl.when(kind == 0)
            def _():
                diagonal(slot_a, slot_b, first)

            @pl.when(count > 0)
            def _():
                def nth(i):
                    return begin + (i + kind * (y + 1)) % count

                def step(i, top_a):
                    n = nth(i)
                    pl.when(i == count - 1)(ahead)
                    top_a = whole(slot_a, slot_b, n, slot_a, nth(jnp.minimum(i + 1, count - 1)), top_a)

                    @pl.when(final)
                    def _():
                        finish(n, 0)
                    return top_a

                lax.fori_loop(0, count, step, put_score(slot_a, nth(0), 0))

            return 0

        lax.fori_loop(0, 8, visit, 0)

    own = pltpu.make_async_copy(obuf.at[y], rows_ref.at[:, head_columns(y)], own_sem.at[4])
    own.start()
    total = part[y]
    for d in (1, 3, 2):
        other = (y + d) % 4
        remote(part.at[y], parts.at[other], p_send.at[y], p_recv.at[other], sibling).wait_recv()
        total = total + parts[other]
    square[...] = total

    def s_copy(d):
        return remote(square, squares.at[15 - d], s_send.at[0], s_recv.at[0], (mine, (tp + d) % 16))

    for d in range(1, 16):
        s_copy(d).start()
    all_sums = remote(squares, squares, s_send.at[0], s_recv.at[0], sibling)
    all_sums.wait_recv()
    total = total + jnp.sum(squares[...], axis=0)
    factor_ref[...] = lax.rsqrt(total * (1.0 / D) + EPSILON)

    own.wait()
    for d in (1, 3, 2):
        other = (y + d) % 4
        remote(obuf.at[y], rows_ref.at[:, head_columns(other)], o_send.at[y], o_recv.at[other], sibling).wait_recv()
        o_copy(other).wait_send()
        p_copy(other).wait_send()

        @pl.when(half == 0)
        def _():
            q_copy(d).wait_send()
    for d in range(1, 16):
        doc_copy(d).wait_send()

    all_sums.wait_send()

    def sent(v, _):
        for a in range(2):
            pass_on(a, mine, fwd_send.at[a, v], sibling).wait_send()
        return 0

    lax.fori_loop(0, 4 + 4 * half, sent, 0)

    @pl.when(half == 0)
    def _():
        for a in range(2):
            pass_on(a, mine, cross_send.at[a, 3], sibling).wait_send()

    @pl.when(half == 1)
    def _():
        for a in range(2):
            kv_copy(a, 2).wait_send()


def fused(queries, keys, values, docs, gain):
    hbm = pl.BlockSpec(memory_space=pltpu.HBM)
    vmem = pl.BlockSpec(memory_space=pltpu.VMEM)
    dma = pltpu.SemaphoreType.DMA
    bf16, f32 = jnp.bfloat16, jnp.float32
    return pl.pallas_call(
        fused_kernel,
        name="fused",
        out_shape=[
            jax.ShapeDtypeStruct((CHUNK, 4 * HEAD_DIM), bf16),
            jax.ShapeDtypeStruct((1, CHUNK), f32),
        ],
        in_specs=[hbm] * 5,
        out_specs=[vmem] * 2,
        scratch_shapes=[
            pltpu.VMEM((1, HEAD_DIM), f32),
            pltpu.VMEM((4, CHUNK, HEAD_DIM), bf16),
            pltpu.VMEM((16, CHUNK, HEAD_DIM), bf16),
            pltpu.VMEM((16, CHUNK, HEAD_DIM), bf16),
            pltpu.VMEM((16, 4, 128), jnp.int32),
            pltpu.VMEM((4, CHUNK, HEAD_DIM), bf16),
            pltpu.VMEM((16, CHUNK, HEAD_DIM), bf16),
            pltpu.VMEM((16, ROWS, CHUNK), bf16),
            pltpu.VMEM((2, CHUNK, CHUNK), f32),
            pltpu.VMEM((4, ROWS, CHUNK), f32),
            pltpu.VMEM((4, 1, CHUNK), f32),
            pltpu.VMEM((4, CHUNK, HEAD_DIM), bf16),
            pltpu.VMEM((4, 1, CHUNK), f32),
            pltpu.VMEM((4, 1, CHUNK), f32),
            pltpu.VMEM((1, CHUNK), f32),
            pltpu.VMEM((15, 1, CHUNK), f32),
            dma((4,)), dma((4,)), dma((2, 4)), dma((2, 16)), dma((2, 8)), dma((2, 4)), dma((16,)), dma((16,)), dma((6,)),
            dma((4,)), dma((4,)), dma((4,)), dma((4,)), dma((16,)), dma((16,)),
        ],
        compiler_params=pltpu.CompilerParams(collective_id=0, has_side_effects=True, vmem_limit_bytes=56 * 10**6),
    )(queries, keys, values, docs, gain)


def local(queries, keys, values, doc_ids, attn_gain):
    docs, gain = doc_ids.reshape(4, 128), attn_gain.reshape(1, 4 * HEAD_DIM)
    docs, gain = (pltpu.with_memory_space_constraint(x, pltpu.HBM) for x in (docs, gain))
    rows, factor = fused(queries, keys, values, docs, gain)
    return (rows.astype(jnp.float32) * factor.reshape(CHUNK, 1)).astype(jnp.bfloat16)


def solution(mesh):
    placed = (P("ctx", "tp"), P("ctx", "tp"), P("ctx", "tp"), P("ctx"), P("tp"))
    return jax.shard_map(
        local, mesh=mesh, in_specs=placed, out_specs=P("ctx", "tp"), check_vma=False
    )
```
